32 devices in a mesh: groups: 2 (over y), wide: 16 (over z, x, core), narrow: 1.
Axes of the slice: x: 2, y: 2, z: 4, core: 2. Of those that a mesh axis runs over, the one named last changes fastest.
Arguments:
- tokens: bfloat16 [2048, 2560], P(('groups', 'wide'), 'narrow'), parts along dimension 0, may hold values from -6 to 6
- expert_ids: int32 [2048, 2], P(('groups', 'wide')), parts along dimension 0, may hold values from 0 to 7, all different within a row; in each aligned block of 64 rows (0 to 63, 64 to 127, ...) at most 32 rows name the same one
- route_weights: float32 [2048, 2], P(('groups', 'wide')), parts along dimension 0, may hold values from 0.1 to 1
- gate_weight: bfloat16 [16, 384, 2560], P('wide', 'narrow'), may hold values from -0.125 to 0.125
- up_weight: bfloat16 [16, 384, 2560], P('wide', 'narrow'), may hold values from -0.125 to 0.125
- down_weight: bfloat16 [16, 384, 2560], P('wide', 'narrow'), may hold values from -0.21875 to 0.21875
Outputs:
- mixed: bfloat16 [2048, 2560], P(('groups', 'wide'), 'narrow'), parts along dimension 0
The draws below stay inside these ranges and needn't reach their ends.
There are 2 independent parts, one for each index of `groups`. The reference program is written for one: setup_inputs(seed, part) draws one part's arguments, and reference() takes and returns one part's arrays. A program takes and returns all parts, laid end to end along the dimension named above; an argument that names none is the same for every part. Nothing has to cross between parts.
Inputs may be any that keep to these rules, and one draw needn't show every extreme that they name: `expert_ids`: each row names 2 different experts. Within the rows of one device (64 tokens along wide) no expert is named more than 32 times, a bound that some block reaches.
All inputs are finite; a program needn't handle non-finite values.
Results may differ from the reference program's by a relative error of at most 0.0057.
Values may be sent and summed in bfloat16 or wider, within the bound.
A program may use at most 64 MiB of HBM per device.

```python
import math
import jax
import jax.numpy as jnp
import numpy as np
from jax import lax

D = 2560
HID = 768
TOPK = 2
TOK_DEV = 64
EXPERTS = 8
CAP = 32
TOKENS = 1024
N_WIDE = 16


def block_scale(own_key, shape, shards, smallest, largest):
    gain = 1.0
    for axis_at, parts in shards:
        draws = jax.random.uniform(jax.random.fold_in(jax.random.fold_in(own_key, 6), axis_at), (parts,), jnp.float32, smallest / len(shards), largest / len(shards))
        gain = gain * jnp.repeat(jnp.exp(draws), shape[axis_at] // parts).reshape((-1,) + (1,) * (len(shape) - 1 - axis_at))
    return gain


def routed_block(stream_key, own, number, rows, count, top, most, skew):
    order = jax.random.permutation(stream_key, count)
    crowded, ordinary = portions_of(count, rows * top, most, skew, True), portions_of(count, rows * top, most, skew, False)
    places = jnp.arange(count)

    def named(lengths, turn):
        used = int((lengths > 0).sum())
        fixed = max(1, used // 4)
        passed = fixed + (places - fixed + turn * (used - fixed)) % max(1, count - fixed)
        return jnp.zeros((count,), jnp.int32).at[order[jnp.where(places < fixed, places, passed)]].set(jnp.asarray(lengths, jnp.int32))

    lengths = jnp.where(number % 4 == 0, named(crowded, number // 4), named(ordinary, number - number // 4 - 1))
    mixed = jax.random.permutation(jax.random.fold_in(own, 3), count)
    giver, sink = mixed[0:count // 2 * 2:2], mixed[1:count // 2 * 2:2]
    room = jnp.minimum(lengths[giver] - 1, most - lengths[sink]) // 2
    room = jnp.where((giver == order[0]) | (sink == order[0]) | (lengths[sink] == 0), 0, jnp.maximum(room, 0))
    passed = jax.random.randint(jax.random.fold_in(own, 4), (count // 2,), 0, 1 << 20) % (room + 1)
    lengths = lengths.at[giver].add(-passed).at[sink].add(passed)
    items = jnp.searchsorted(jnp.cumsum(lengths), jnp.arange(rows * top), side="right").astype(jnp.int32)
    table = items.reshape(top, rows).T
    table = table[jax.random.permutation(jax.random.fold_in(own, 1), rows)]
    turn = jax.random.randint(jax.random.fold_in(own, 2), (rows, 1), 0, top)
    return jnp.take_along_axis(table, (jnp.arange(top)[None, :] + turn) % top, axis=1)


def portions_of(number_of, total, bound, skew, full):
    loads = [(1 << 20) // math.isqrt(grade ** skew) + 1 for grade in range(1, number_of + 1)]
    largest = bound if full else min(bound, max(-(-total // number_of), total * loads[0] // sum(loads)))
    least = 1 if total - largest >= number_of - 1 else 0
    given, rest = [largest] + [least] * (number_of - 1), total - largest - least * (number_of - 1)
    while rest > 0:
        free = [i for i in range(1, number_of) if given[i] < largest] or [i for i in range(1, number_of) if given[i] < bound]
        mass, budget = sum([loads[i] for i in free]), rest
        for i in free:
            addition = min(bound - given[i], max(1, budget * loads[i] // mass), rest)
            given[i] = given[i] + addition
            rest = rest - addition
    return np.array(given)


def normal_values(rng, shape, deviation, bound, cuts=(), kind=jnp.bfloat16):
    loudness = block_scale(rng, shape, cuts, -0.22, 0.18) if cuts else 1.0
    drawn = jax.random.normal(rng, shape, jnp.float32) * deviation * loudness
    return jnp.minimum(jnp.maximum(drawn, -bound), bound).astype(kind)


def setup_inputs(seed: int = 0, part: int = 0) -> dict:
    arg_keys = jax.random.split(jax.random.key(seed), 7)
    own_keys = jax.random.split(jax.random.fold_in(arg_keys[6], part), 7)
    tokens = normal_values(own_keys[0], (TOKENS, D), 1.0, 6.0, ((0, 16),))
    expert_ids_keys = jax.random.split(jax.random.fold_in(own_keys[1], 1), TOKENS // TOK_DEV)
    expert_ids_turns = jax.random.permutation(jax.random.fold_in(own_keys[1], 3), TOKENS // TOK_DEV)
    expert_ids = jax.vmap(lambda own, number: routed_block(jax.random.fold_in(own_keys[1], 2), own, number, TOK_DEV, EXPERTS, TOPK, CAP, 2))(expert_ids_keys, expert_ids_turns).reshape((TOKENS, TOPK))
    route_weights = jnp.clip(0.1 + 0.9 * jax.random.uniform(own_keys[2], (TOKENS, TOPK), jnp.float32) ** block_scale(own_keys[2], (TOKENS, TOPK), ((0, 16),), -0.2, 0.2), 0.1, 1.0)
    gate_weight = normal_values(arg_keys[3], (2 * EXPERTS, HID // 2, D), D ** -0.5, 0.125, ((0, 16),))
    up_weight = normal_values(arg_keys[4], (2 * EXPERTS, HID // 2, D), D ** -0.5, 0.125, ((0, 16),))
    down_weight = normal_values(arg_keys[5], (2 * EXPERTS, HID // 2, D), HID ** -0.5, 0.21875, ((0, 16),))
    return dict(tokens=tokens, expert_ids=expert_ids, route_weights=route_weights, gate_weight=gate_weight, up_weight=up_weight, down_weight=down_weight)


def expert_quarters(rows, gate_full, up_full, down_full):
    quarter_size = HID // 4
    total = jnp.zeros((rows.shape[0], D), jnp.float32)
    for quarter in range(4):
        low = quarter * quarter_size
        high = low + quarter_size
        gate = jnp.dot(rows, gate_full[low:high].T, preferred_element_type=jnp.float32)
        up_part = jnp.dot(rows, up_full[low:high].T, preferred_element_type=jnp.float32)
        hidden = (jax.nn.silu(gate) * up_part).astype(jnp.bfloat16)
        total = total + jnp.dot(hidden, down_full[low:high], preferred_element_type=jnp.float32)
    return total


def reference(tokens, expert_ids, route_weights, gate_weight, up_weight, down_weight):
    pair_count = TOKENS * TOPK
    most_rows = N_WIDE * CAP
    flat_ids = expert_ids.reshape(-1)
    padded_weights = jnp.concatenate([route_weights.reshape(-1), jnp.zeros((1,), jnp.float32)])
    padded_tokens = jnp.concatenate([tokens, jnp.zeros((1, D), jnp.bfloat16)], axis=0)

    def add_expert(output, expert):
        chosen = jnp.nonzero(flat_ids == expert, size=most_rows, fill_value=pair_count)[0].astype(jnp.int32)
        token_rows = jnp.where(chosen < pair_count, chosen // TOPK, TOKENS).astype(jnp.int32)
        rows = padded_tokens[token_rows]
        start = (2 * expert).astype(jnp.int32)
        gate_full = lax.dynamic_slice_in_dim(gate_weight, start, 2, 0).reshape(HID, D)
        up_full = lax.dynamic_slice_in_dim(up_weight, start, 2, 0).reshape(HID, D)
        down_full = lax.dynamic_slice_in_dim(down_weight, start, 2, 0).reshape(HID, D)
        total = expert_quarters(rows, gate_full, up_full, down_full)
        rounded = lax.optimization_barrier(total.astype(jnp.bfloat16))
        scaled = rounded.astype(jnp.float32) * padded_weights[chosen][:, None]
        output = output.at[token_rows].add(scaled, mode="drop")
        return output, None

    output, unused = lax.scan(add_expert, jnp.zeros((TOKENS, D), jnp.float32), jnp.arange(EXPERTS, dtype=jnp.int32))
    return output.astype(jnp.bfloat16)
```

```python
import functools

import jax
import jax.numpy as jnp
from jax import lax
from jax.experimental import pallas as pl
from jax.experimental.pallas import tpu as pltpu
from jax.sharding import PartitionSpec as P

F32 = jnp.float32
BF16 = jnp.bfloat16


def per_device(tokens, expert_ids, route_weights, gate_weight, up_weight, down_weight):
    tok_rows = tokens.shape[0]
    picks = expert_ids.shape[1]
    width_wide = lax.axis_size("wide")
    experts = width_wide // 2
    slots = 4 * tok_rows * picks // width_wide
    payload = lax.all_gather(tokens, "narrow", axis=1, tiled=True)
    feature_width = payload.shape[1]
    flat_ids = expert_ids.reshape(-1)
    flat_weights = route_weights.reshape(-1)
    onehot = (flat_ids[:, None] == jnp.arange(experts, dtype=jnp.int32)[None, :]).astype(jnp.int32)
    slot_rank = jnp.sum(jnp.cumsum(onehot, axis=0) * onehot, axis=1) - 1
    slot_place = flat_ids * slots + slot_rank
    token_source = jnp.arange(tok_rows * picks, dtype=jnp.int32) // picks
    slot_token = jnp.full((experts * slots,), tok_rows, jnp.int32).at[slot_place].set(token_source)
    padded = jnp.concatenate([payload, jnp.zeros((1, feature_width), payload.dtype)], axis=0)
    buffer = padded[slot_token].reshape(experts, slots, feature_width)
    outgoing = jnp.repeat(buffer, 2, axis=0)
    received = lax.all_to_all(outgoing, "wide", split_axis=0, concat_axis=0, tiled=True)
    model_width = received.shape[2]
    rows = received.reshape(width_wide * slots, model_width)
    gate = jnp.einsum("rd,hd->rh", rows, gate_weight[0], preferred_element_type=jnp.float32)
    up_part = jnp.einsum("rd,hd->rh", rows, up_weight[0], preferred_element_type=jnp.float32)
    hidden = (jax.nn.silu(gate) * up_part).astype(jnp.bfloat16)
    quarter_out = jnp.dot(hidden, down_weight[0], preferred_element_type=jnp.float32)
    quarter_blocks = quarter_out.reshape(width_wide, slots, model_width)
    returned = lax.all_to_all(quarter_blocks, "wide", split_axis=0, concat_axis=0, tiled=True)
    by_expert = jnp.sum(returned.reshape(experts, 2, slots, model_width), axis=1)
    pieces = by_expert[flat_ids, slot_rank]
    expert_total = lax.psum_scatter(pieces, "narrow", scatter_dimension=1, tiled=True)
    rounded = lax.optimization_barrier(expert_total.astype(jnp.bfloat16))
    pair_total = rounded.astype(jnp.float32) * flat_weights[:, None]
    column_width = pair_total.shape[1]
    mixed = jnp.sum(pair_total.reshape(tok_rows, picks, column_width), axis=1)
    return mixed.astype(jnp.bfloat16)


def flip(number, mask, bits):
    out = number
    for b in range(bits):
        if (mask >> b) & 1:
            bit = lax.rem(lax.div(number, 1 << b), 2)
            out = out + (1 - 2 * bit) * (1 << b)
    return out


def kernel(chips, slots, groups_of, tok, ids, rw, gw, uw, dw, out,
           sendbuf, recvbuf, outbuf, retbuf, gbuf, ubuf, dbuf, hid,
           local_sem, w_send, w_recv, d_send, d_recv, r_send, r_recv):
    bits = chips.bit_length() - 1
    half = gw.shape[1]
    width = tok.shape[1]
    toks = tok.shape[0]
    cols = chips * slots
    tile = 512
    me = lax.axis_index("wide")
    chip = lax.div(me, 2)
    core = lax.rem(me, 2)
    sibling = 2 * chip + 1 - core
    partner = [flip(chip, r, bits) for r in range(chips)]
    device = [2 * p + core for p in partner]

    barrier = pltpu.get_barrier_semaphore()
    pl.semaphore_signal(barrier, inc=1, device_id={"wide": sibling}, device_id_type=pl.DeviceIdType.MESH)
    for r in range(1, chips):
        pl.semaphore_signal(barrier, inc=1, device_id={"wide": device[r]}, device_id_type=pl.DeviceIdType.MESH)

    pairs = ((gw, gbuf), (uw, ubuf), (dw, dbuf))
    local = [pltpu.make_async_copy(src.at[0], dst.at[pl.ds(0, half)], local_sem.at[i])
             for i, (src, dst) in enumerate(pairs)]
    for c in local:
        c.start()

    col = lax.broadcasted_iota(jnp.int32, (toks, cols), 1)
    expert = jnp.zeros((toks, cols), jnp.int32)
    first = jnp.zeros((toks, cols), jnp.int32)
    for r in range(chips):
        inside = (col >= r * slots) & (col < (r + 1) * slots)
        expert = jnp.where(inside, partner[r], expert)
        first = jnp.where(inside, r * slots, first)
    pick0 = jnp.where(ids[:, 0:1] == expert, 1.0, 0.0)
    pick1 = jnp.where(ids[:, 1:2] == expert, 1.0, 0.0)
    named = pick0 + pick1
    before = jnp.where(lax.broadcasted_iota(jnp.int32, (toks, toks), 0)
                       > lax.broadcasted_iota(jnp.int32, (toks, toks), 1), 1.0, 0.0)
    rank = jnp.dot(before.astype(BF16), named.astype(BF16), preferred_element_type=F32)
    here = jnp.where(rank == (col - first).astype(F32), 1.0, 0.0)
    choose = jnp.transpose(here * named).astype(BF16)
    pick0 = (here * pick0).astype(BF16)
    pick1 = (here * pick1).astype(BF16)

    for at in range(0, width, tile):
        picked = jnp.dot(choose, tok[:, at:at + tile], preferred_element_type=F32).astype(BF16)
        sendbuf[:, at:at + tile] = picked
        recvbuf[0:slots, at:at + tile] = picked[0:slots]

    pl.semaphore_wait(barrier, chips)

    dispatch, back = [None], [None]
    for r in range(1, chips):
        span = pl.ds(r * slots, slots)
        dispatch.append(pltpu.make_async_remote_copy(
            src_ref=sendbuf.at[span], dst_ref=recvbuf.at[span], send_sem=d_send.at[r], recv_sem=d_recv.at[r],
            device_id={"wide": device[r]}, device_id_type=pl.DeviceIdType.MESH))
        back.append(pltpu.make_async_remote_copy(
            src_ref=outbuf.at[span], dst_ref=retbuf.at[span], send_sem=r_send.at[r], recv_sem=r_recv.at[r],
            device_id={"wide": device[r]}, device_id_type=pl.DeviceIdType.MESH))
    for r in range(chips - 1, 0, -1):
        dispatch[r].start()
    remote = [pltpu.make_async_remote_copy(
        src_ref=src.at[0], dst_ref=dst.at[pl.ds(half, half)], send_sem=w_send.at[i], recv_sem=w_recv.at[i],
        device_id={"wide": sibling}, device_id_type=pl.DeviceIdType.MESH) for i, (src, dst) in enumerate(pairs)]
    for c in remote:
        c.start()
    for c in local:
        c.wait()
    for c in remote:
        c.wait_recv()

    hid_tile = 256
    for low, high in groups_of:
        for r in range(max(low, 1), high):
            dispatch[r].wait_recv()
        base, rows = low * slots, (high - low) * slots

        @pl.loop(0, 2 * half // hid_tile)
        def _(i):
            at = pl.ds(pl.multiple_of(i * hid_tile, hid_tile), hid_tile)
            x = recvbuf[base:base + rows, :]
            dims = (((1,), (1,)), ((), ()))
            gate = lax.dot_general(x, gbuf[at, :], dims, preferred_element_type=F32)
            up = lax.dot_general(x, ubuf[at, :], dims, preferred_element_type=F32)
            hid[base:base + rows, at] = (gate / (1.0 + jnp.exp(-gate)) * up).astype(BF16)

        @pl.loop(0, width // tile)
        def _(i):
            at = pl.ds(pl.multiple_of(i * tile, tile), tile)
            part = jnp.dot(hid[base:base + rows, :], dbuf[:, at], preferred_element_type=F32)
            outbuf[base:base + rows, at] = part.astype(BF16)

        for r in range(max(low, 1), high):
            back[r].start()

    retbuf[0:slots, :] = outbuf[0:slots, :]
    for r in range(1, chips):
        back[r].wait_recv()
    for at in range(0, width, tile):
        part = retbuf[:, at:at + tile]
        total = (rw[:, 0:1] * jnp.dot(pick0, part, preferred_element_type=F32)
                 + rw[:, 1:2] * jnp.dot(pick1, part, preferred_element_type=F32))
        out[:, at:at + tile] = total.astype(BF16)

    for c in remote:
        c.wait_send()
    for r in range(1, chips):
        dispatch[r].wait_send()
        back[r].wait_send()


def fused(tokens, expert_ids, route_weights, gate_weight, up_weight, down_weight):
    toks, width = tokens.shape
    wide = lax.axis_size("wide")
    chips = wide // 2
    slots = 4 * toks * expert_ids.shape[1] // wide
    half = gate_weight.shape[1]
    rows = chips * slots
    near = chips // 2
    groups_of = ((0, near), (near, near + near // 2), (near + near // 2, chips))
    vmem = pl.BlockSpec(memory_space=pltpu.VMEM)
    hbm = pl.BlockSpec(memory_space=pl.ANY)
    return pl.pallas_call(
        functools.partial(kernel, chips, slots, groups_of),
        out_shape=jax.ShapeDtypeStruct((toks, width), BF16),
        in_specs=[vmem, vmem, vmem, hbm, hbm, hbm],
        out_specs=vmem,
        scratch_shapes=[pltpu.VMEM((rows, width), BF16)] * 4
        + [pltpu.VMEM((2 * half, width), BF16)] * 3
        + [pltpu.VMEM((rows, 2 * half), BF16)]
        + [pltpu.SemaphoreType.DMA((3,))] * 3
        + [pltpu.SemaphoreType.DMA((chips,))] * 4,
        compiler_params=pltpu.CompilerParams(
            collective_id=0, has_side_effects=True, vmem_limit_bytes=48 * 1024 * 1024),
        cost_estimate=pl.CostEstimate(
            flops=12 * rows * half * width, bytes_accessed=6 * half * width + 4 * toks * width,
            transcendentals=2 * rows * half),
    )(tokens, expert_ids, route_weights, gate_weight, up_weight, down_weight)


def solution(mesh):
    in_specs = (
        P(("groups", "wide"), "narrow"),
        P(("groups", "wide"), None),
        P(("groups", "wide"), None),
        P("wide", "narrow", None),
        P("wide", "narrow", None),
        P("wide", "narrow", None),
    )
    out_specs = P(("groups", "wide"), "narrow")
    chips = mesh.shape["wide"] // 2
    whole_rows = mesh.shape["narrow"] == 1 and chips >= 4 and chips & (chips - 1) == 0
    return jax.shard_map(
        fused if whole_rows else per_device, mesh=mesh, in_specs=in_specs, out_specs=out_specs, check_vma=False
    )
```

```python
import functools

import jax
import jax.numpy as jnp
from jax import lax
from jax.experimental import pallas as pl
from jax.experimental.pallas import tpu as pltpu
from jax.sharding import PartitionSpec as P

F32 = jnp.float32
BF16 = jnp.bfloat16


def per_device(tokens, expert_ids, route_weights, gate_weight, up_weight, down_weight):
    tok_rows = tokens.shape[0]
    picks = expert_ids.shape[1]
    width_wide = lax.axis_size("wide")
    experts = width_wide // 2
    slots = 4 * tok_rows * picks // width_wide
    payload = lax.all_gather(tokens, "narrow", axis=1, tiled=True)
    feature_width = payload.shape[1]
    flat_ids = expert_ids.reshape(-1)
    flat_weights = route_weights.reshape(-1)
    onehot = (flat_ids[:, None] == jnp.arange(experts, dtype=jnp.int32)[None, :]).astype(jnp.int32)
    slot_rank = jnp.sum(jnp.cumsum(onehot, axis=0) * onehot, axis=1) - 1
    slot_place = flat_ids * slots + slot_rank
    token_source = jnp.arange(tok_rows * picks, dtype=jnp.int32) // picks
    slot_token = jnp.full((experts * slots,), tok_rows, jnp.int32).at[slot_place].set(token_source)
    padded = jnp.concatenate([payload, jnp.zeros((1, feature_width), payload.dtype)], axis=0)
    buffer = padded[slot_token].reshape(experts, slots, feature_width)
    outgoing = jnp.repeat(buffer, 2, axis=0)
    received = lax.all_to_all(outgoing, "wide", split_axis=0, concat_axis=0, tiled=True)
    model_width = received.shape[2]
    rows = received.reshape(width_wide * slots, model_width)
    gate = jnp.einsum("rd,hd->rh", rows, gate_weight[0], preferred_element_type=jnp.float32)
    up_part = jnp.einsum("rd,hd->rh", rows, up_weight[0], preferred_element_type=jnp.float32)
    hidden = (jax.nn.silu(gate) * up_part).astype(jnp.bfloat16)
    quarter_out = jnp.dot(hidden, down_weight[0], preferred_element_type=jnp.float32)
    quarter_blocks = quarter_out.reshape(width_wide, slots, model_width)
    returned = lax.all_to_all(quarter_blocks, "wide", split_axis=0, concat_axis=0, tiled=True)
    by_expert = jnp.sum(returned.reshape(experts, 2, slots, model_width), axis=1)
    pieces = by_expert[flat_ids, slot_rank]
    expert_total = lax.psum_scatter(pieces, "narrow", scatter_dimension=1, tiled=True)
    rounded = lax.optimization_barrier(expert_total.astype(jnp.bfloat16))
    pair_total = rounded.astype(jnp.float32) * flat_weights[:, None]
    column_width = pair_total.shape[1]
    mixed = jnp.sum(pair_total.reshape(tok_rows, picks, column_width), axis=1)
    return mixed.astype(jnp.bfloat16)


def flip(number, mask, bits):
    out = number
    for b in range(bits):
        if (mask >> b) & 1:
            bit = lax.rem(lax.div(number, 1 << b), 2)
            out = out + (1 - 2 * bit) * (1 << b)
    return out


def column(row):
    n = row.shape[1]
    same = lax.broadcasted_iota(jnp.int32, (n, n), 0) == lax.broadcasted_iota(jnp.int32, (n, n), 1)
    return jnp.sum(jnp.where(same, row, 0.0), axis=1, keepdims=True)


def one_hots(ids, experts, slots):
    toks = ids.shape[1]
    cols = len(experts) * slots
    id0 = column(ids[0:1, :].astype(F32))
    id1 = column(ids[1:2, :].astype(F32))
    col = lax.broadcasted_iota(jnp.int32, (toks, cols), 1)
    expert = jnp.zeros((toks, cols), F32)
    first = jnp.zeros((toks, cols), jnp.int32)
    for r, e in enumerate(experts):
        inside = (col >= r * slots) & (col < (r + 1) * slots)
        expert = jnp.where(inside, e.astype(F32), expert)
        first = jnp.where(inside, r * slots, first)
    pick0 = jnp.where(id0 == expert, 1.0, 0.0)
    pick1 = jnp.where(id1 == expert, 1.0, 0.0)
    named = pick0 + pick1
    before = jnp.where(lax.broadcasted_iota(jnp.int32, (toks, toks), 0)
                       > lax.broadcasted_iota(jnp.int32, (toks, toks), 1), 1.0, 0.0)
    rank = jnp.dot(before.astype(BF16), named.astype(BF16), preferred_element_type=F32)
    here = jnp.where(rank == (col - first).astype(F32), 1.0, 0.0)
    choose = jnp.transpose(here * named).astype(BF16)
    return choose, (here * pick0).astype(BF16), (here * pick1).astype(BF16)


def kernel(chips, slots, tile, tok, ids, rw, gw, uw, dw, out,
           tokbuf, idbuf, rwbuf, fartok, farid, farrw, nearsend, relaysend, recvbuf, outbuf,
           nearret, farret, mixfar, mixback, nearsum, gbuf, ubuf, dbuf, hid,
           local_sem, w_send, w_recv, t_send, t_recv, m_send, m_recv, n_send, n_recv,
           l_send, l_recv, b_send, b_recv, f_send, f_recv, c_send, c_recv):
    bits = chips.bit_length() - 1
    near = chips // 2
    half = gw.shape[1]
    width = tok.shape[1]
    chunks = width // tile
    mine = near * slots
    me = lax.axis_index("wide")
    chip = lax.div(me, 2)
    core = lax.rem(me, 2)
    sibling = 2 * chip + 1 - core
    partner = [flip(chip, r, bits) for r in range(near)]
    device = [2 * p + core for p in partner]
    across = 2 * flip(chip, near, bits) + core

    def remote(src, dst, send, recv, to):
        return pltpu.make_async_remote_copy(src_ref=src, dst_ref=dst, send_sem=send, recv_sem=recv,
                                            device_id={"wide": to}, device_id_type=pl.DeviceIdType.MESH)

    barrier = pltpu.get_barrier_semaphore()
    for to in [across, sibling] + device[1:]:
        pl.semaphore_signal(barrier, inc=1, device_id={"wide": to}, device_id_type=pl.DeviceIdType.MESH)

    pairs = ((gw, gbuf), (uw, ubuf), (dw, dbuf))
    small = [pltpu.make_async_copy(src, dst, local_sem.at[3 + i])
             for i, (src, dst) in enumerate(((ids, idbuf), (rw, rwbuf), (tok, tokbuf)))]
    local = [pltpu.make_async_copy(src.at[0], dst.at[pl.ds(0, half)], local_sem.at[i])
             for i, (src, dst) in enumerate(pairs)]
    for c in small + local:
        c.start()
    for c in small:
        c.wait()

    choose, near0, near1 = one_hots(idbuf, partner, slots)
    for c in range(chunks):
        cut = slice(c * tile, (c + 1) * tile)
        picked = jnp.dot(choose, tokbuf[:, cut], preferred_element_type=F32).astype(BF16)
        nearsend[:, cut] = picked
        recvbuf[0:slots, cut] = picked[0:slots]

    pl.semaphore_wait(barrier, near + 1)

    span = [pl.ds(r * slots, slots) for r in range(chips)]
    cuts = [pl.ds(c * tile, tile) for c in range(chunks)]
    meta = [remote(idbuf, farid, m_send.at[0], m_recv.at[0], across),
            remote(rwbuf, farrw, m_send.at[1], m_recv.at[1], across)]
    over = [remote(tokbuf.at[:, cuts[c]], fartok.at[:, cuts[c]], t_send.at[c], t_recv.at[c], across)
            for c in range(chunks)]
    swap = [remote(src.at[0], dst.at[pl.ds(half, half)], w_send.at[i], w_recv.at[i], sibling)
            for i, (src, dst) in enumerate(pairs)]
    direct = [remote(nearsend.at[span[r]], recvbuf.at[span[r]], n_send.at[r], n_recv.at[r], device[r])
              for r in range(1, near)]
    relay = [[remote(relaysend.at[span[r], cuts[c]], recvbuf.at[span[near + r], cuts[c]],
                     l_send.at[r, c], l_recv.at[r, c], device[r]) for r in range(1, near)] for c in range(chunks)]
    back = [remote(outbuf.at[span[r]], nearret.at[span[r]], b_send.at[r], b_recv.at[r], device[r])
            for r in range(1, near)]
    farback = [[remote(outbuf.at[span[near + r], cuts[c]], farret.at[span[r], cuts[c]],
                       f_send.at[r, c], f_recv.at[r, c], device[r]) for r in range(1, near)] for c in range(chunks)]
    home = [remote(mixfar.at[:, cuts[c]], mixback.at[:, cuts[c]], c_send.at[c], c_recv.at[c], across)
            for c in range(chunks)]

    for c in meta + over + swap + direct:
        c.start()

    for c in meta:
        c.wait_recv()
    choose, far0, far1 = one_hots(farid, partner, slots)
    for c in range(chunks):
        cut = slice(c * tile, (c + 1) * tile)
        over[c].wait_recv()
        picked = jnp.dot(choose, fartok[:, cut], preferred_element_type=F32).astype(BF16)
        relaysend[:, cut] = picked
        recvbuf[mine:mine + slots, cut] = picked[0:slots]
        for copy in relay[c]:
            copy.start()

    for c in local:
        c.wait()
    for c in swap:
        c.wait_recv()

    hid_tile = 256

    def into_hidden(base):
        @pl.loop(0, 2 * half // hid_tile)
        def _(i):
            at = pl.ds(pl.multiple_of(i * hid_tile, hid_tile), hid_tile)
            x = recvbuf[base:base + mine, :]
            dims = (((1,), (1,)), ((), ()))
            gate = lax.dot_general(x, gbuf[at, :], dims, preferred_element_type=F32)
            up = lax.dot_general(x, ubuf[at, :], dims, preferred_element_type=F32)
            hid[:, at] = (gate / (1.0 + jnp.exp(-gate)) * up).astype(BF16)

    for c in direct:
        c.wait_recv()
    into_hidden(0)
    for c in range(chunks):
        cut = slice(c * tile, (c + 1) * tile)
        part = jnp.dot(hid[...], dbuf[:, cut], preferred_element_type=F32).astype(BF16)
        outbuf[0:mine, cut] = part
        nearret[0:slots, cut] = part[0:slots]
    for c in back:
        c.start()

    for c in range(chunks):
        for copy in relay[c]:
            copy.wait_recv()
    into_hidden(mine)
    for c in range(chunks):
        cut = slice(c * tile, (c + 1) * tile)
        part = jnp.dot(hid[...], dbuf[:, cut], preferred_element_type=F32).astype(BF16)
        outbuf[mine:2 * mine, cut] = part
        farret[0:slots, cut] = part[0:slots]
        for copy in farback[c]:
            copy.start()

    w0, w1 = column(farrw[0:1, :]), column(farrw[1:2, :])
    for c in range(chunks):
        cut = slice(c * tile, (c + 1) * tile)
        for copy in farback[c]:
            copy.wait_recv()
        part = farret[:, cut]
        mixfar[:, cut] = (w0 * jnp.dot(far0, part, preferred_element_type=F32)
                          + w1 * jnp.dot(far1, part, preferred_element_type=F32)).astype(BF16)
        home[c].start()

    w0, w1 = column(rwbuf[0:1, :]), column(rwbuf[1:2, :])
    for c in back:
        c.wait_recv()
    for c in range(chunks):
        cut = slice(c * tile, (c + 1) * tile)
        part = nearret[:, cut]
        nearsum[:, cut] = (w0 * jnp.dot(near0, part, preferred_element_type=F32)
                           + w1 * jnp.dot(near1, part, preferred_element_type=F32))
    for c in range(chunks):
        cut = slice(c * tile, (c + 1) * tile)
        home[c].wait_recv()
        out[:, cut] = (nearsum[:, cut] + mixback[:, cut].astype(F32)).astype(BF16)

    for c in meta + over + swap + direct + back + home:
        c.wait_send()
    for c in range(chunks):
        for copy in relay[c] + farback[c]:
            copy.wait_send()


def fused(tokens, expert_ids, route_weights, gate_weight, up_weight, down_weight):
    toks, width = tokens.shape
    picks = expert_ids.shape[1]
    wide = lax.axis_size("wide")
    chips = wide // 2
    near = chips // 2
    slots = 4 * toks * picks // wide
    half = gate_weight.shape[1]
    rows = chips * slots
    mine = near * slots
    tile = 512
    chunks = width // tile
    vmem = pl.BlockSpec(memory_space=pltpu.VMEM)
    hbm = pl.BlockSpec(memory_space=pl.ANY)
    tok_like = pltpu.VMEM((toks, width), BF16)
    near_like = pltpu.VMEM((mine, width), BF16)
    all_like = pltpu.VMEM((rows, width), BF16)
    id_like = pltpu.VMEM((picks, toks), jnp.int32)
    rw_like = pltpu.VMEM((picks, toks), F32)
    sems = pltpu.SemaphoreType.DMA
    return pl.pallas_call(
        functools.partial(kernel, chips, slots, tile),
        out_shape=jax.ShapeDtypeStruct((toks, width), BF16),
        in_specs=[hbm] * 6,
        out_specs=vmem,
        scratch_shapes=[tok_like, id_like, rw_like, tok_like, id_like, rw_like, near_like, near_like,
                        all_like, all_like, near_like, near_like, tok_like, tok_like,
                        pltpu.VMEM((toks, width), F32)]
        + [pltpu.VMEM((2 * half, width), BF16)] * 3
        + [pltpu.VMEM((mine, 2 * half), BF16)]
        + [sems((6,)), sems((3,)), sems((3,)), sems((chunks,)), sems((chunks,)), sems((2,)), sems((2,)),
           sems((near,)), sems((near,)), sems((near, chunks)), sems((near, chunks)),
           sems((near,)), sems((near,)), sems((near, chunks)), sems((near, chunks)),
           sems((chunks,)), sems((chunks,))],
        compiler_params=pltpu.CompilerParams(
            collective_id=0, has_side_effects=True, vmem_limit_bytes=60 * 1024 * 1024),
        cost_estimate=pl.CostEstimate(
            flops=12 * rows * half * width, bytes_accessed=6 * half * width + 4 * toks * width,
            transcendentals=2 * rows * half),
    )(tokens, expert_ids.T, route_weights.T, gate_weight, up_weight, down_weight)


def solution(mesh):
    in_specs = (
        P(("groups", "wide"), "narrow"),
        P(("groups", "wide"), None),
        P(("groups", "wide"), None),
        P("wide", "narrow", None),
        P("wide", "narrow", None),
        P("wide", "narrow", None),
    )
    out_specs = P(("groups", "wide"), "narrow")
    chips = mesh.shape["wide"] // 2
    whole_rows = mesh.shape["narrow"] == 1 and chips >= 4 and chips & (chips - 1) == 0
    return jax.shard_map(
        fused if whole_rows else per_device, mesh=mesh, in_specs=in_specs, out_specs=out_specs, check_vma=False
    )
```

```python
import functools

import jax
import jax.numpy as jnp
from jax import lax
from jax.experimental import pallas as pl
from jax.experimental.pallas import tpu as pltpu
from jax.sharding import PartitionSpec as P

F32 = jnp.float32
BF16 = jnp.bfloat16


def per_device(tokens, expert_ids, route_weights, gate_weight, up_weight, down_weight):
    tok_rows = tokens.shape[0]
    picks = expert_ids.shape[1]
    width_wide = lax.axis_size("wide")
    experts = width_wide // 2
    slots = 4 * tok_rows * picks // width_wide
    payload = lax.all_gather(tokens, "narrow", axis=1, tiled=True)
    feature_width = payload.shape[1]
    flat_ids = expert_ids.reshape(-1)
    flat_weights = route_weights.reshape(-1)
    onehot = (flat_ids[:, None] == jnp.arange(experts, dtype=jnp.int32)[None, :]).astype(jnp.int32)
    slot_rank = jnp.sum(jnp.cumsum(onehot, axis=0) * onehot, axis=1) - 1
    slot_place = flat_ids * slots + slot_rank
    token_source = jnp.arange(tok_rows * picks, dtype=jnp.int32) // picks
    slot_token = jnp.full((experts * slots,), tok_rows, jnp.int32).at[slot_place].set(token_source)
    padded = jnp.concatenate([payload, jnp.zeros((1, feature_width), payload.dtype)], axis=0)
    buffer = padded[slot_token].reshape(experts, slots, feature_width)
    outgoing = jnp.repeat(buffer, 2, axis=0)
    received = lax.all_to_all(outgoing, "wide", split_axis=0, concat_axis=0, tiled=True)
    model_width = received.shape[2]
    rows = received.reshape(width_wide * slots, model_width)
    gate = jnp.einsum("rd,hd->rh", rows, gate_weight[0], preferred_element_type=jnp.float32)
    up_part = jnp.einsum("rd,hd->rh", rows, up_weight[0], preferred_element_type=jnp.float32)
    hidden = (jax.nn.silu(gate) * up_part).astype(jnp.bfloat16)
    quarter_out = jnp.dot(hidden, down_weight[0], preferred_element_type=jnp.float32)
    quarter_blocks = quarter_out.reshape(width_wide, slots, model_width)
    returned = lax.all_to_all(quarter_blocks, "wide", split_axis=0, concat_axis=0, tiled=True)
    by_expert = jnp.sum(returned.reshape(experts, 2, slots, model_width), axis=1)
    pieces = by_expert[flat_ids, slot_rank]
    expert_total = lax.psum_scatter(pieces, "narrow", scatter_dimension=1, tiled=True)
    rounded = lax.optimization_barrier(expert_total.astype(jnp.bfloat16))
    pair_total = rounded.astype(jnp.float32) * flat_weights[:, None]
    column_width = pair_total.shape[1]
    mixed = jnp.sum(pair_total.reshape(tok_rows, picks, column_width), axis=1)
    return mixed.astype(jnp.bfloat16)


def flip(number, mask, bits):
    out = number
    for b in range(bits):
        if (mask >> b) & 1:
            bit = lax.rem(lax.div(number, 1 << b), 2)
            out = out + (1 - 2 * bit) * (1 << b)
    return out


def column(row):
    n = row.shape[1]
    same = lax.broadcasted_iota(jnp.int32, (n, n), 0) == lax.broadcasted_iota(jnp.int32, (n, n), 1)
    return jnp.sum(jnp.where(same, row, 0.0), axis=1, keepdims=True)


def one_hots(ids, experts, slots):
    toks = ids.shape[1]
    cols = len(experts) * slots
    id0 = column(ids[0:1, :].astype(F32))
    id1 = column(ids[1:2, :].astype(F32))
    col = lax.broadcasted_iota(jnp.int32, (toks, cols), 1)
    expert = jnp.zeros((toks, cols), F32)
    first = jnp.zeros((toks, cols), jnp.int32)
    for r, e in enumerate(experts):
        inside = (col >= r * slots) & (col < (r + 1) * slots)
        expert = jnp.where(inside, e.astype(F32), expert)
        first = jnp.where(inside, r * slots, first)
    pick0 = jnp.where(id0 == expert, 1.0, 0.0)
    pick1 = jnp.where(id1 == expert, 1.0, 0.0)
    named = pick0 + pick1
    before = jnp.where(lax.broadcasted_iota(jnp.int32, (toks, toks), 0)
                       > lax.broadcasted_iota(jnp.int32, (toks, toks), 1), 1.0, 0.0)
    rank = jnp.dot(before.astype(BF16), named.astype(BF16), preferred_element_type=F32)
    here = jnp.where(rank == (col - first).astype(F32), 1.0, 0.0)
    choose = jnp.transpose(here * named).astype(BF16)
    return choose, (here * pick0).astype(BF16), (here * pick1).astype(BF16)


def kernel(chips, slots, tile, tok, ids, rw, gw, uw, dw, out,
           tokbuf, idbuf, rwbuf, fartok, farid, farrw, nearsend, relaysend, recvbuf, outbuf,
           nearret, farret, mixfar, mixback, nearsum, gbuf, ubuf, dbuf, hid,
           local_sem, w_send, w_recv, t_send, t_recv, m_send, m_recv, n_send, n_recv,
           l_send, l_recv, b_send, b_recv, f_send, f_recv, c_send, c_recv):
    bits = chips.bit_length() - 1
    near = chips // 2
    half = gw.shape[1]
    width = tok.shape[1]
    chunks = width // tile
    mine = near * slots
    me = lax.axis_index("wide")
    chip = lax.div(me, 2)
    core = lax.rem(me, 2)
    sibling = 2 * chip + 1 - core
    partner = [flip(chip, r, bits) for r in range(near)]
    device = [2 * p + core for p in partner]
    across = 2 * flip(chip, near, bits) + core

    def remote(src, dst, send, recv, to):
        return pltpu.make_async_remote_copy(src_ref=src, dst_ref=dst, send_sem=send, recv_sem=recv,
                                            device_id={"wide": to}, device_id_type=pl.DeviceIdType.MESH)

    barrier = pltpu.get_barrier_semaphore()
    for to in [across, sibling] + device[1:]:
        pl.semaphore_signal(barrier, inc=1, device_id={"wide": to}, device_id_type=pl.DeviceIdType.MESH)

    pairs = ((gw, gbuf), (uw, ubuf), (dw, dbuf))
    small = [pltpu.make_async_copy(src, dst, local_sem.at[3 + i])
             for i, (src, dst) in enumerate(((ids, idbuf), (rw, rwbuf), (tok, tokbuf)))]
    local = [pltpu.make_async_copy(src.at[0], dst.at[pl.ds(0, half)], local_sem.at[i])
             for i, (src, dst) in enumerate(pairs)]
    for c in small + local:
        c.start()

    span = [pl.ds(r * slots, slots) for r in range(chips)]
    cuts = [pl.ds(c * tile, tile) for c in range(chunks)]
    meta = [remote(ids, farid, m_send.at[0], m_recv.at[0], across),
            remote(rw, farrw, m_send.at[1], m_recv.at[1], across)]
    over = [remote(tok.at[:, cuts[c]], fartok.at[:, cuts[c]], t_send.at[c], t_recv.at[c], across)
            for c in range(chunks)]
    swap = [remote(src.at[0], dst.at[pl.ds(half, half)], w_send.at[i], w_recv.at[i], sibling)
            for i, (src, dst) in enumerate(pairs)]
    direct = [remote(nearsend.at[span[r]], recvbuf.at[span[r]], n_send.at[r], n_recv.at[r], device[r])
              for r in range(1, near)]
    relay = [[remote(relaysend.at[span[r], cuts[c]], recvbuf.at[span[near + r], cuts[c]],
                     l_send.at[r, c], l_recv.at[r, c], device[r]) for r in range(1, near)] for c in range(chunks)]
    back = [remote(outbuf.at[span[r]], nearret.at[span[r]], b_send.at[r], b_recv.at[r], device[r])
            for r in range(1, near)]
    farback = [[remote(outbuf.at[span[near + r], cuts[c]], farret.at[span[r], cuts[c]],
                       f_send.at[r, c], f_recv.at[r, c], device[r]) for r in range(1, near)] for c in range(chunks)]
    home = [remote(mixfar.at[:, cuts[c]], mixback.at[:, cuts[c]], c_send.at[c], c_recv.at[c], across)
            for c in range(chunks)]

    pl.semaphore_wait(barrier, near + 1)
    for c in meta + over:
        c.start()

    for c in small:
        c.wait()
    choose, near0, near1 = one_hots(idbuf, partner, slots)
    for c in range(chunks):
        cut = slice(c * tile, (c + 1) * tile)
        picked = jnp.dot(choose, tokbuf[:, cut], preferred_element_type=F32).astype(BF16)
        nearsend[:, cut] = picked
        recvbuf[0:slots, cut] = picked[0:slots]
    for c in direct + swap:
        c.start()

    for c in meta:
        c.wait_recv()
    choose, far0, far1 = one_hots(farid, partner, slots)
    for c in range(chunks):
        cut = slice(c * tile, (c + 1) * tile)
        over[c].wait_recv()
        picked = jnp.dot(choose, fartok[:, cut], preferred_element_type=F32).astype(BF16)
        relaysend[:, cut] = picked
        recvbuf[mine:mine + slots, cut] = picked[0:slots]
        for copy in relay[c]:
            copy.start()

    for c in local:
        c.wait()
    for c in swap:
        c.wait_recv()

    hid_tile = 256

    def into_hidden(base):
        @pl.loop(0, 2 * half // hid_tile)
        def _(i):
            at = pl.ds(pl.multiple_of(i * hid_tile, hid_tile), hid_tile)
            x = recvbuf[base:base + mine, :]
            dims = (((1,), (1,)), ((), ()))
            gate = lax.dot_general(x, gbuf[at, :], dims, preferred_element_type=F32)
            up = lax.dot_general(x, ubuf[at, :], dims, preferred_element_type=F32)
            hid[:, at] = (gate / (1.0 + jnp.exp(-gate)) * up).astype(BF16)

    for c in direct:
        c.wait_recv()
    into_hidden(0)
    for c in range(chunks):
        cut = slice(c * tile, (c + 1) * tile)
        part = jnp.dot(hid[...], dbuf[:, cut], preferred_element_type=F32).astype(BF16)
        outbuf[0:mine, cut] = part
        nearret[0:slots, cut] = part[0:slots]
    for c in back:
        c.start()

    for c in range(chunks):
        for copy in relay[c]:
            copy.wait_recv()
    into_hidden(mine)
    for c in range(chunks):
        cut = slice(c * tile, (c + 1) * tile)
        part = jnp.dot(hid[...], dbuf[:, cut], preferred_element_type=F32).astype(BF16)
        outbuf[mine:2 * mine, cut] = part
        farret[0:slots, cut] = part[0:slots]
        for copy in farback[c]:
            copy.start()

    w0, w1 = column(farrw[0:1, :]), column(farrw[1:2, :])
    for c in range(chunks):
        cut = slice(c * tile, (c + 1) * tile)
        for copy in farback[c]:
            copy.wait_recv()
        part = farret[:, cut]
        mixfar[:, cut] = (w0 * jnp.dot(far0, part, preferred_element_type=F32)
                          + w1 * jnp.dot(far1, part, preferred_element_type=F32)).astype(BF16)
        home[c].start()

    w0, w1 = column(rwbuf[0:1, :]), column(rwbuf[1:2, :])
    for c in back:
        c.wait_recv()
    for c in range(chunks):
        cut = slice(c * tile, (c + 1) * tile)
        part = nearret[:, cut]
        nearsum[:, cut] = (w0 * jnp.dot(near0, part, preferred_element_type=F32)
                           + w1 * jnp.dot(near1, part, preferred_element_type=F32))
    for c in range(chunks):
        cut = slice(c * tile, (c + 1) * tile)
        home[c].wait_recv()
        out[:, cut] = (nearsum[:, cut] + mixback[:, cut].astype(F32)).astype(BF16)

    for c in meta + over + swap + direct + back + home:
        c.wait_send()
    for c in range(chunks):
        for copy in relay[c] + farback[c]:
            copy.wait_send()


def fused(tokens, expert_ids, route_weights, gate_weight, up_weight, down_weight):
    toks, width = tokens.shape
    picks = expert_ids.shape[1]
    wide = lax.axis_size("wide")
    chips = wide // 2
    near = chips // 2
    slots = 4 * toks * picks // wide
    half = gate_weight.shape[1]
    rows = chips * slots
    mine = near * slots
    tile = 512
    chunks = width // tile
    vmem = pl.BlockSpec(memory_space=pltpu.VMEM)
    hbm = pl.BlockSpec(memory_space=pl.ANY)
    tok_like = pltpu.VMEM((toks, width), BF16)
    near_like = pltpu.VMEM((mine, width), BF16)
    all_like = pltpu.VMEM((rows, width), BF16)
    id_like = pltpu.VMEM((picks, toks), jnp.int32)
    rw_like = pltpu.VMEM((picks, toks), F32)
    sems = pltpu.SemaphoreType.DMA
    return pl.pallas_call(
        functools.partial(kernel, chips, slots, tile),
        out_shape=jax.ShapeDtypeStruct((toks, width), BF16),
        in_specs=[hbm] * 6,
        out_specs=vmem,
        scratch_shapes=[tok_like, id_like, rw_like, tok_like, id_like, rw_like, near_like, near_like,
                        all_like, all_like, near_like, near_like, tok_like, tok_like,
                        pltpu.VMEM((toks, width), F32)]
        + [pltpu.VMEM((2 * half, width), BF16)] * 3
        + [pltpu.VMEM((mine, 2 * half), BF16)]
        + [sems((6,)), sems((3,)), sems((3,)), sems((chunks,)), sems((chunks,)), sems((2,)), sems((2,)),
           sems((near,)), sems((near,)), sems((near, chunks)), sems((near, chunks)),
           sems((near,)), sems((near,)), sems((near, chunks)), sems((near, chunks)),
           sems((chunks,)), sems((chunks,))],
        compiler_params=pltpu.CompilerParams(
            collective_id=0, has_side_effects=True, vmem_limit_bytes=60 * 1024 * 1024),
        cost_estimate=pl.CostEstimate(
            flops=12 * rows * half * width, bytes_accessed=6 * half * width + 4 * toks * width,
            transcendentals=2 * rows * half),
    )(tokens, expert_ids.T, route_weights.T, gate_weight, up_weight, down_weight)


def solution(mesh):
    in_specs = (
        P(("groups", "wide"), "narrow"),
        P(("groups", "wide"), None),
        P(("groups", "wide"), None),
        P("wide", "narrow", None),
        P("wide", "narrow", None),
        P("wide", "narrow", None),
    )
    out_specs = P(("groups", "wide"), "narrow")
    chips = mesh.shape["wide"] // 2
    whole_rows = mesh.shape["narrow"] == 1 and chips >= 4 and chips & (chips - 1) == 0
    return jax.shard_map(
        fused if whole_rows else per_device, mesh=mesh, in_specs=in_specs, out_specs=out_specs, check_vma=False
    )
```

```python
import functools

import jax
import jax.numpy as jnp
from jax import lax
from jax.experimental import pallas as pl
from jax.experimental.pallas import tpu as pltpu
from jax.sharding import PartitionSpec as P

F32 = jnp.float32
BF16 = jnp.bfloat16


def per_device(tokens, expert_ids, route_weights, gate_weight, up_weight, down_weight):
    tok_rows = tokens.shape[0]
    picks = expert_ids.shape[1]
    width_wide = lax.axis_size("wide")
    experts = width_wide // 2
    slots = 4 * tok_rows * picks // width_wide
    payload = lax.all_gather(tokens, "narrow", axis=1, tiled=True)
    feature_width = payload.shape[1]
    flat_ids = expert_ids.reshape(-1)
    flat_weights = route_weights.reshape(-1)
    onehot = (flat_ids[:, None] == jnp.arange(experts, dtype=jnp.int32)[None, :]).astype(jnp.int32)
    slot_rank = jnp.sum(jnp.cumsum(onehot, axis=0) * onehot, axis=1) - 1
    slot_place = flat_ids * slots + slot_rank
    token_source = jnp.arange(tok_rows * picks, dtype=jnp.int32) // picks
    slot_token = jnp.full((experts * slots,), tok_rows, jnp.int32).at[slot_place].set(token_source)
    padded = jnp.concatenate([payload, jnp.zeros((1, feature_width), payload.dtype)], axis=0)
    buffer = padded[slot_token].reshape(experts, slots, feature_width)
    outgoing = jnp.repeat(buffer, 2, axis=0)
    received = lax.all_to_all(outgoing, "wide", split_axis=0, concat_axis=0, tiled=True)
    model_width = received.shape[2]
    rows = received.reshape(width_wide * slots, model_width)
    gate = jnp.einsum("rd,hd->rh", rows, gate_weight[0], preferred_element_type=jnp.float32)
    up_part = jnp.einsum("rd,hd->rh", rows, up_weight[0], preferred_element_type=jnp.float32)
    hidden = (jax.nn.silu(gate) * up_part).astype(jnp.bfloat16)
    quarter_out = jnp.dot(hidden, down_weight[0], preferred_element_type=jnp.float32)
    quarter_blocks = quarter_out.reshape(width_wide, slots, model_width)
    returned = lax.all_to_all(quarter_blocks, "wide", split_axis=0, concat_axis=0, tiled=True)
    by_expert = jnp.sum(returned.reshape(experts, 2, slots, model_width), axis=1)
    pieces = by_expert[flat_ids, slot_rank]
    expert_total = lax.psum_scatter(pieces, "narrow", scatter_dimension=1, tiled=True)
    rounded = lax.optimization_barrier(expert_total.astype(jnp.bfloat16))
    pair_total = rounded.astype(jnp.float32) * flat_weights[:, None]
    column_width = pair_total.shape[1]
    mixed = jnp.sum(pair_total.reshape(tok_rows, picks, column_width), axis=1)
    return mixed.astype(jnp.bfloat16)


def flip(number, mask, bits):
    out = number
    for b in range(bits):
        if (mask >> b) & 1:
            bit = lax.rem(lax.div(number, 1 << b), 2)
            out = out + (1 - 2 * bit) * (1 << b)
    return out


def column(row):
    n = row.shape[1]
    same = lax.broadcasted_iota(jnp.int32, (n, n), 0) == lax.broadcasted_iota(jnp.int32, (n, n), 1)
    return jnp.sum(jnp.where(same, row, 0.0), axis=1, keepdims=True)


def one_hots(ids, experts, slots):
    toks = ids.shape[1]
    cols = len(experts) * slots
    id0 = column(ids[0:1, :].astype(F32))
    id1 = column(ids[1:2, :].astype(F32))
    col = lax.broadcasted_iota(jnp.int32, (toks, cols), 1)
    expert = jnp.zeros((toks, cols), F32)
    first = jnp.zeros((toks, cols), jnp.int32)
    for r, e in enumerate(experts):
        inside = (col >= r * slots) & (col < (r + 1) * slots)
        expert = jnp.where(inside, e.astype(F32), expert)
        first = jnp.where(inside, r * slots, first)
    pick0 = jnp.where(id0 == expert, 1.0, 0.0)
    pick1 = jnp.where(id1 == expert, 1.0, 0.0)
    named = pick0 + pick1
    before = jnp.where(lax.broadcasted_iota(jnp.int32, (toks, toks), 0)
                       > lax.broadcasted_iota(jnp.int32, (toks, toks), 1), 1.0, 0.0)
    rank = jnp.dot(before.astype(BF16), named.astype(BF16), preferred_element_type=F32)
    here = jnp.where(rank == (col - first).astype(F32), 1.0, 0.0)
    choose = jnp.transpose(here * named).astype(BF16)
    return choose, (here * pick0).astype(BF16), (here * pick1).astype(BF16)


def kernel(chips, slots, tile, tok, ids, rw, gw, uw, dw, out,
           tokbuf, idbuf, rwbuf, fartok, farid, farrw, nearsend, relaysend, recvbuf, outbuf,
           nearret, farret, mixfar, mixback, nearsum, gbuf, ubuf, dbuf, hid,
           local_sem, w_send, w_recv, t_send, t_recv, m_send, m_recv, n_send, n_recv,
           l_send, l_recv, b_send, b_recv, f_send, f_recv, c_send, c_recv):
    bits = chips.bit_length() - 1
    near = chips // 2
    half = gw.shape[1]
    width = tok.shape[1]
    chunks = width // tile
    mine = near * slots
    me = lax.axis_index("wide")
    chip = lax.div(me, 2)
    core = lax.rem(me, 2)
    sibling = 2 * chip + 1 - core
    partner = [flip(chip, r, bits) for r in range(near)]
    device = [2 * p + core for p in partner]
    across = 2 * flip(chip, near, bits) + core

    def remote(src, dst, send, recv, to):
        return pltpu.make_async_remote_copy(src_ref=src, dst_ref=dst, send_sem=send, recv_sem=recv,
                                            device_id={"wide": to}, device_id_type=pl.DeviceIdType.MESH)

    barrier = pltpu.get_barrier_semaphore()
    for to in [across, sibling] + device[1:]:
        pl.semaphore_signal(barrier, inc=1, device_id={"wide": to}, device_id_type=pl.DeviceIdType.MESH)

    pairs = ((gw, gbuf), (uw, ubuf), (dw, dbuf))
    small = [pltpu.make_async_copy(src, dst, local_sem.at[3 + i])
             for i, (src, dst) in enumerate(((ids, idbuf), (rw, rwbuf), (tok, tokbuf)))]
    local = [pltpu.make_async_copy(src.at[0], dst.at[pl.ds(0, half)], local_sem.at[i])
             for i, (src, dst) in enumerate(pairs)]
    for c in small + local:
        c.start()

    span = [pl.ds(r * slots, slots) for r in range(chips)]
    cuts = [pl.ds(c * tile, tile) for c in range(chunks)]
    meta = [remote(ids, farid, m_send.at[0], m_recv.at[0], across),
            remote(rw, farrw, m_send.at[1], m_recv.at[1], across)]
    over = [remote(tok.at[:, cuts[c]], fartok.at[:, cuts[c]], t_send.at[c], t_recv.at[c], across)
            for c in range(chunks)]
    swap = [remote(src.at[0], dst.at[pl.ds(half, half)], w_send.at[i], w_recv.at[i], sibling)
            for i, (src, dst) in enumerate(pairs)]
    direct = [remote(nearsend.at[span[r]], recvbuf.at[span[r]], n_send.at[r], n_recv.at[r], device[r])
              for r in range(1, near)]
    relay = [[remote(relaysend.at[span[r], cuts[c]], recvbuf.at[span[near + r], cuts[c]],
                     l_send.at[r, c], l_recv.at[r, c], device[r]) for r in range(1, near)] for c in range(chunks)]
    back = [remote(outbuf.at[span[r]], nearret.at[span[r]], b_send.at[r], b_recv.at[r], device[r])
            for r in range(1, near)]
    farback = [[remote(outbuf.at[span[near + r], cuts[c]], farret.at[span[r], cuts[c]],
                       f_send.at[r, c], f_recv.at[r, c], device[r]) for r in range(1, near)] for c in range(chunks)]
    home = [remote(mixfar.at[:, cuts[c]], mixback.at[:, cuts[c]], c_send.at[c], c_recv.at[c], across)
            for c in range(chunks)]

    pl.semaphore_wait(barrier, near + 1)
    for c in meta + over:
        c.start()

    for c in small:
        c.wait()
    choose, near0, near1 = one_hots(idbuf, partner, slots)
    for c in range(chunks):
        cut = slice(c * tile, (c + 1) * tile)
        picked = jnp.dot(choose, tokbuf[:, cut], preferred_element_type=F32).astype(BF16)
        nearsend[:, cut] = picked
        recvbuf[0:slots, cut] = picked[0:slots]
    for c in direct + swap:
        c.start()

    for c in meta:
        c.wait_recv()
    choose, far0, far1 = one_hots(farid, partner, slots)
    for c in range(chunks):
        cut = slice(c * tile, (c + 1) * tile)
        over[c].wait_recv()
        picked = jnp.dot(choose, fartok[:, cut], preferred_element_type=F32).astype(BF16)
        relaysend[:, cut] = picked
        recvbuf[mine:mine + slots, cut] = picked[0:slots]
        for copy in relay[c]:
            copy.start()

    for c in local:
        c.wait()
    for c in swap:
        c.wait_recv()

    hid_tile = 256

    def into_hidden(base):
        @pl.loop(0, 2 * half // hid_tile)
        def _(i):
            at = pl.ds(pl.multiple_of(i * hid_tile, hid_tile), hid_tile)
            x = recvbuf[base:base + mine, :]
            dims = (((1,), (1,)), ((), ()))
            gate = lax.dot_general(x, gbuf[at, :], dims, preferred_element_type=F32)
            up = lax.dot_general(x, ubuf[at, :], dims, preferred_element_type=F32)
            hid[:, at] = (gate / (1.0 + jnp.exp(-gate)) * up).astype(BF16)

    for c in direct:
        c.wait_recv()
    into_hidden(0)
    for c in range(chunks):
        cut = slice(c * tile, (c + 1) * tile)
        part = jnp.dot(hid[...], dbuf[:, cut], preferred_element_type=F32).astype(BF16)
        outbuf[0:mine, cut] = part
        nearret[0:slots, cut] = part[0:slots]
    for c in back:
        c.start()

    for c in range(chunks):
        for copy in relay[c]:
            copy.wait_recv()
    into_hidden(mine)
    for c in range(chunks):
        cut = slice(c * tile, (c + 1) * tile)
        part = jnp.dot(hid[...], dbuf[:, cut], preferred_element_type=F32).astype(BF16)
        outbuf[mine:2 * mine, cut] = part
        farret[0:slots, cut] = part[0:slots]
        for copy in farback[c]:
            copy.start()

    w0, w1 = column(farrw[0:1, :]), column(farrw[1:2, :])
    for c in range(chunks):
        cut = slice(c * tile, (c + 1) * tile)
        for copy in farback[c]:
            copy.wait_recv()
        part = farret[:, cut]
        mixfar[:, cut] = (w0 * jnp.dot(far0, part, preferred_element_type=F32)
                          + w1 * jnp.dot(far1, part, preferred_element_type=F32)).astype(BF16)
        home[c].start()

    w0, w1 = column(rwbuf[0:1, :]), column(rwbuf[1:2, :])
    for c in back:
        c.wait_recv()
    for c in range(chunks):
        cut = slice(c * tile, (c + 1) * tile)
        part = nearret[:, cut]
        nearsum[:, cut] = (w0 * jnp.dot(near0, part, preferred_element_type=F32)
                           + w1 * jnp.dot(near1, part, preferred_element_type=F32))
    for c in range(chunks):
        cut = slice(c * tile, (c + 1) * tile)
        home[c].wait_recv()
        out[:, cut] = (nearsum[:, cut] + mixback[:, cut].astype(F32)).astype(BF16)

    for c in meta + over + swap + direct + back + home:
        c.wait_send()
    for c in range(chunks):
        for copy in relay[c] + farback[c]:
            copy.wait_send()


def fused(tokens, expert_ids, route_weights, gate_weight, up_weight, down_weight):
    toks, width = tokens.shape
    picks = expert_ids.shape[1]
    wide = lax.axis_size("wide")
    chips = wide // 2
    near = chips // 2
    slots = 4 * toks * picks // wide
    half = gate_weight.shape[1]
    rows = chips * slots
    mine = near * slots
    tile = 256
    chunks = width // tile
    vmem = pl.BlockSpec(memory_space=pltpu.VMEM)
    hbm = pl.BlockSpec(memory_space=pl.ANY)
    tok_like = pltpu.VMEM((toks, width), BF16)
    near_like = pltpu.VMEM((mine, width), BF16)
    all_like = pltpu.VMEM((rows, width), BF16)
    id_like = pltpu.VMEM((picks, toks), jnp.int32)
    rw_like = pltpu.VMEM((picks, toks), F32)
    sems = pltpu.SemaphoreType.DMA
    return pl.pallas_call(
        functools.partial(kernel, chips, slots, tile),
        out_shape=jax.ShapeDtypeStruct((toks, width), BF16),
        in_specs=[hbm] * 6,
        out_specs=vmem,
        scratch_shapes=[tok_like, id_like, rw_like, tok_like, id_like, rw_like, near_like, near_like,
                        all_like, all_like, near_like, near_like, tok_like, tok_like,
                        pltpu.VMEM((toks, width), F32)]
        + [pltpu.VMEM((2 * half, width), BF16)] * 3
        + [pltpu.VMEM((mine, 2 * half), BF16)]
        + [sems((6,)), sems((3,)), sems((3,)), sems((chunks,)), sems((chunks,)), sems((2,)), sems((2,)),
           sems((near,)), sems((near,)), sems((near, chunks)), sems((near, chunks)),
           sems((near,)), sems((near,)), sems((near, chunks)), sems((near, chunks)),
           sems((chunks,)), sems((chunks,))],
        compiler_params=pltpu.CompilerParams(
            collective_id=0, has_side_effects=True, vmem_limit_bytes=60 * 1024 * 1024),
        cost_estimate=pl.CostEstimate(
            flops=12 * rows * half * width, bytes_accessed=6 * half * width + 4 * toks * width,
            transcendentals=2 * rows * half),
    )(tokens, expert_ids.T, route_weights.T, gate_weight, up_weight, down_weight)


def solution(mesh):
    in_specs = (
        P(("groups", "wide"), "narrow"),
        P(("groups", "wide"), None),
        P(("groups", "wide"), None),
        P("wide", "narrow", None),
        P("wide", "narrow", None),
        P("wide", "narrow", None),
    )
    out_specs = P(("groups", "wide"), "narrow")
    chips = mesh.shape["wide"] // 2
    whole_rows = mesh.shape["narrow"] == 1 and chips >= 4 and chips & (chips - 1) == 0
    return jax.shard_map(
        fused if whole_rows else per_device, mesh=mesh, in_specs=in_specs, out_specs=out_specs, check_vma=False
    )
```

```python
import functools

import jax
import jax.numpy as jnp
from jax import lax
from jax.experimental import pallas as pl
from jax.experimental.pallas import tpu as pltpu
from jax.sharding import PartitionSpec as P

F32 = jnp.float32
BF16 = jnp.bfloat16


def per_device(tokens, expert_ids, route_weights, gate_weight, up_weight, down_weight):
    tok_rows = tokens.shape[0]
    picks = expert_ids.shape[1]
    width_wide = lax.axis_size("wide")
    experts = width_wide // 2
    slots = 4 * tok_rows * picks // width_wide
    payload = lax.all_gather(tokens, "narrow", axis=1, tiled=True)
    feature_width = payload.shape[1]
    flat_ids = expert_ids.reshape(-1)
    flat_weights = route_weights.reshape(-1)
    onehot = (flat_ids[:, None] == jnp.arange(experts, dtype=jnp.int32)[None, :]).astype(jnp.int32)
    slot_rank = jnp.sum(jnp.cumsum(onehot, axis=0) * onehot, axis=1) - 1
    slot_place = flat_ids * slots + slot_rank
    token_source = jnp.arange(tok_rows * picks, dtype=jnp.int32) // picks
    slot_token = jnp.full((experts * slots,), tok_rows, jnp.int32).at[slot_place].set(token_source)
    padded = jnp.concatenate([payload, jnp.zeros((1, feature_width), payload.dtype)], axis=0)
    buffer = padded[slot_token].reshape(experts, slots, feature_width)
    outgoing = jnp.repeat(buffer, 2, axis=0)
    received = lax.all_to_all(outgoing, "wide", split_axis=0, concat_axis=0, tiled=True)
    model_width = received.shape[2]
    rows = received.reshape(width_wide * slots, model_width)
    gate = jnp.einsum("rd,hd->rh", rows, gate_weight[0], preferred_element_type=jnp.float32)
    up_part = jnp.einsum("rd,hd->rh", rows, up_weight[0], preferred_element_type=jnp.float32)
    hidden = (jax.nn.silu(gate) * up_part).astype(jnp.bfloat16)
    quarter_out = jnp.dot(hidden, down_weight[0], preferred_element_type=jnp.float32)
    quarter_blocks = quarter_out.reshape(width_wide, slots, model_width)
    returned = lax.all_to_all(quarter_blocks, "wide", split_axis=0, concat_axis=0, tiled=True)
    by_expert = jnp.sum(returned.reshape(experts, 2, slots, model_width), axis=1)
    pieces = by_expert[flat_ids, slot_rank]
    expert_total = lax.psum_scatter(pieces, "narrow", scatter_dimension=1, tiled=True)
    rounded = lax.optimization_barrier(expert_total.astype(jnp.bfloat16))
    pair_total = rounded.astype(jnp.float32) * flat_weights[:, None]
    column_width = pair_total.shape[1]
    mixed = jnp.sum(pair_total.reshape(tok_rows, picks, column_width), axis=1)
    return mixed.astype(jnp.bfloat16)


def flip(number, mask, bits):
    out = number
    for b in range(bits):
        if (mask >> b) & 1:
            bit = lax.rem(lax.div(number, 1 << b), 2)
            out = out + (1 - 2 * bit) * (1 << b)
    return out


def column(row):
    n = row.shape[1]
    same = lax.broadcasted_iota(jnp.int32, (n, n), 0) == lax.broadcasted_iota(jnp.int32, (n, n), 1)
    return jnp.sum(jnp.where(same, row, 0.0), axis=1, keepdims=True)


def one_hots(ids, experts, slots):
    toks = ids.shape[1]
    cols = len(experts) * slots
    id0 = column(ids[0:1, :].astype(F32))
    id1 = column(ids[1:2, :].astype(F32))
    col = lax.broadcasted_iota(jnp.int32, (toks, cols), 1)
    expert = jnp.zeros((toks, cols), F32)
    first = jnp.zeros((toks, cols), jnp.int32)
    for r, e in enumerate(experts):
        inside = (col >= r * slots) & (col < (r + 1) * slots)
        expert = jnp.where(inside, e.astype(F32), expert)
        first = jnp.where(inside, r * slots, first)
    pick0 = jnp.where(id0 == expert, 1.0, 0.0)
    pick1 = jnp.where(id1 == expert, 1.0, 0.0)
    named = pick0 + pick1
    before = jnp.where(lax.broadcasted_iota(jnp.int32, (toks, toks), 0)
                       > lax.broadcasted_iota(jnp.int32, (toks, toks), 1), 1.0, 0.0)
    rank = jnp.dot(before.astype(BF16), named.astype(BF16), preferred_element_type=F32)
    here = jnp.where(rank == (col - first).astype(F32), 1.0, 0.0)
    choose = jnp.transpose(here * named).astype(BF16)
    return choose, (here * pick0).astype(BF16), (here * pick1).astype(BF16)


def kernel(slots, tile, tok, ids, rw, gw, uw, dw, out,
           tokbuf, idbuf, rwbuf, fartok, farid, farrw, nearsend, relaysend, recvbuf, outbuf,
           nearret, farret, mixfar, mixback, nearsum, gbuf, ubuf, dbuf, hid,
           local_sem, w_send, w_recv, t_send, t_recv, m_send, m_recv, n_send, n_recv,
           l_send, l_recv, b_send, b_recv, f_send, f_recv, c_send, c_recv):
    near = 4
    half = gw.shape[1]
    width = tok.shape[1]
    chunks = width // tile
    mine = near * slots
    me = lax.axis_index("wide")
    chip = lax.div(me, 2)
    core = lax.rem(me, 2)
    z = lax.div(chip, 2)
    inner = lax.rem(z + 1, 4) >= 2
    outer = lax.rem(z + 1, 4) < 2
    slot = jnp.where(inner, 0, 1)
    sibling = 2 * chip + 1 - core
    partner = [flip(chip, r, 3) for r in range(near)]
    device = [2 * p + core for p in partner]
    across = [2 * flip(chip, 6, 3) + core, 2 * flip(chip, 4, 3) + core]
    relay_of_me = jnp.where(inner, across[0], across[1])

    def remote(src, dst, send, recv, to):
        return pltpu.make_async_remote_copy(src_ref=src, dst_ref=dst, send_sem=send, recv_sem=recv,
                                            device_id={"wide": to}, device_id_type=pl.DeviceIdType.MESH)

    barrier = pltpu.get_barrier_semaphore()
    for to in across + [sibling] + device[1:]:
        pl.semaphore_signal(barrier, inc=1, device_id={"wide": to}, device_id_type=pl.DeviceIdType.MESH)

    pairs = ((gw, gbuf), (uw, ubuf), (dw, dbuf))
    small = [pltpu.make_async_copy(src, dst, local_sem.at[3 + i])
             for i, (src, dst) in enumerate(((ids, idbuf), (rw, rwbuf), (tok, tokbuf)))]
    local = [pltpu.make_async_copy(src.at[0], dst.at[pl.ds(0, half)], local_sem.at[i])
             for i, (src, dst) in enumerate(pairs)]
    for c in small + local:
        c.start()

    span = [pl.ds(r * slots, slots) for r in range(2 * near)]
    cuts = [pl.ds(c * tile, tile) for c in range(chunks)]
    sides = range(2)

    def crossing(at):
        meta = [remote(ids, farid.at[at], m_send.at[0], m_recv.at[at, 0], relay_of_me),
                remote(rw, farrw.at[at], m_send.at[1], m_recv.at[at, 1], relay_of_me)]
        return meta, [remote(tok.at[:, cuts[c]], fartok.at[at, :, cuts[c]], t_send.at[c], t_recv.at[at, c],
                             relay_of_me) for c in range(chunks)]

    meta, over = crossing(slot)
    arriving = [crossing(g) for g in sides]
    swap = [remote(src.at[0], dst.at[pl.ds(half, half)], w_send.at[i], w_recv.at[i], sibling)
            for i, (src, dst) in enumerate(pairs)]
    direct = [remote(nearsend.at[span[r]], recvbuf.at[span[r]], n_send.at[r], n_recv.at[r], device[r])
              for r in range(1, near)]
    back = [remote(outbuf.at[span[r]], nearret.at[span[r]], b_send.at[r], b_recv.at[r], device[r])
            for r in range(1, near)]

    def block(g, i):
        return span[near + 2 * g + i]

    relay = [[[remote(relaysend.at[g, span[r], cuts[c]], recvbuf.at[block(g, r % 2), cuts[c]],
                      l_send.at[g, r, c], l_recv.at[g, r % 2, c], device[r]) for r in (2, 3, 1)]
              for c in range(chunks)] for g in sides]
    answer = [[[None] + [remote(outbuf.at[block(g, r % 2), cuts[c]], farret.at[g, span[r], cuts[c]],
                                f_send.at[g, r % 2, c], f_recv.at[g, r, c], device[r]) for r in range(1, near)]
               for c in range(chunks)] for g in sides]
    home = [[remote(mixfar.at[g, :, cuts[c]], mixback.at[:, cuts[c]], c_send.at[g, c], c_recv.at[c], across[g])
             for c in range(chunks)] for g in sides]

    pl.semaphore_wait(barrier, near + 2)

    @pl.when(inner)
    def _():
        for c in meta + over:
            c.start()

    for c in small:
        c.wait()
    choose, near0, near1 = one_hots(idbuf, partner, slots)
    for c in range(chunks):
        cut = slice(c * tile, (c + 1) * tile)
        picked = jnp.dot(choose, tokbuf[:, cut], preferred_element_type=F32).astype(BF16)
        nearsend[:, cut] = picked
        recvbuf[0:slots, cut] = picked[0:slots]
    for c in direct:
        c.start()

    @pl.when(outer)
    def _():
        for c in meta + over:
            c.start()

    for c in swap:
        c.start()

    @pl.when(inner)
    def _():
        for g in sides:
            for c in arriving[g][0]:
                c.wait_recv()
            choose, unused0, unused1 = one_hots(farid.at[g], partner, slots)
            for c in range(chunks):
                cut = slice(c * tile, (c + 1) * tile)
                arriving[g][1][c].wait_recv()
                picked = jnp.dot(choose, fartok[g, :, cut], preferred_element_type=F32).astype(BF16)
                relaysend[g, :, cut] = picked
                low = mine + 2 * g * slots
                recvbuf[low:low + slots, cut] = picked[0:slots]
                for copy in relay[g][c]:
                    copy.start()

    for c in local:
        c.wait()
    for c in swap:
        c.wait_recv()

    hid_tile = 256

    def into_hidden(base, rows):
        @pl.loop(0, 2 * half // hid_tile)
        def _(i):
            at = pl.ds(pl.multiple_of(i * hid_tile, hid_tile), hid_tile)
            x = recvbuf[base:base + rows, :]
            dims = (((1,), (1,)), ((), ()))
            gate = lax.dot_general(x, gbuf[at, :], dims, preferred_element_type=F32)
            up = lax.dot_general(x, ubuf[at, :], dims, preferred_element_type=F32)
            hid[0:rows, at] = (gate / (1.0 + jnp.exp(-gate)) * up).astype(BF16)

    for c in direct:
        c.wait_recv()
    into_hidden(0, mine)
    for c in range(chunks):
        cut = slice(c * tile, (c + 1) * tile)
        part = jnp.dot(hid[...], dbuf[:, cut], preferred_element_type=F32).astype(BF16)
        outbuf[0:mine, cut] = part
        nearret[0:slots, cut] = part[0:slots]
    for c in back:
        c.start()

    for g in sides:
        low = mine + 2 * g * slots

        @pl.when(outer)
        def _():
            for c in range(chunks):
                relay[g][c][0].wait_recv()

        for c in range(chunks):
            relay[g][c][2].wait_recv()
        into_hidden(low, 2 * slots)
        for c in range(chunks):
            cut = slice(c * tile, (c + 1) * tile)
            part = jnp.dot(hid[0:2 * slots, :], dbuf[:, cut], preferred_element_type=F32).astype(BF16)
            outbuf[low:low + 2 * slots, cut] = part
            farret[g, 0:slots, cut] = part[0:slots]

            @pl.when(inner)
            def _():
                answer[g][c][1].start()

            @pl.when(outer)
            def _():
                answer[g][c][2].start()
                answer[g][c][3].start()

    @pl.when(inner)
    def _():
        for g in sides:
            unused, far0, far1 = one_hots(farid.at[g], partner, slots)
            w0, w1 = column(farrw[g, 0:1, :]), column(farrw[g, 1:2, :])
            for c in range(chunks):
                cut = slice(c * tile, (c + 1) * tile)
                for r in range(1, near):
                    answer[g][c][r].wait_recv()
                part = farret[g, :, cut]
                mixfar[g, :, cut] = (w0 * jnp.dot(far0, part, preferred_element_type=F32)
                                     + w1 * jnp.dot(far1, part, preferred_element_type=F32)).astype(BF16)
                home[g][c].start()

    w0, w1 = column(rwbuf[0:1, :]), column(rwbuf[1:2, :])
    for c in back:
        c.wait_recv()
    for c in range(chunks):
        cut = slice(c * tile, (c + 1) * tile)
        part = nearret[:, cut]
        nearsum[:, cut] = (w0 * jnp.dot(near0, part, preferred_element_type=F32)
                           + w1 * jnp.dot(near1, part, preferred_element_type=F32))
    for c in range(chunks):
        cut = slice(c * tile, (c + 1) * tile)
        home[0][c].wait_recv()
        out[:, cut] = (nearsum[:, cut] + mixback[:, cut].astype(F32)).astype(BF16)

    for c in meta + over + swap + direct + back:
        c.wait_send()

    @pl.when(inner)
    def _():
        for g in sides:
            for c in range(chunks):
                for copy in relay[g][c]:
                    copy.wait_send()
                answer[g][c][1].wait_send()
                home[g][c].wait_send()

    @pl.when(outer)
    def _():
        for g in sides:
            for c in range(chunks):
                answer[g][c][2].wait_send()
                answer[g][c][3].wait_send()


def fused(tokens, expert_ids, route_weights, gate_weight, up_weight, down_weight):
    toks, width = tokens.shape
    picks = expert_ids.shape[1]
    wide = lax.axis_size("wide")
    chips = wide // 2
    near = chips // 2
    slots = 4 * toks * picks // wide
    half = gate_weight.shape[1]
    rows = chips * slots
    mine = near * slots
    tile = 512
    chunks = width // tile
    vmem = pl.BlockSpec(memory_space=pltpu.VMEM)
    hbm = pl.BlockSpec(memory_space=pl.ANY)
    tok_like = pltpu.VMEM((toks, width), BF16)
    near_like = pltpu.VMEM((mine, width), BF16)
    all_like = pltpu.VMEM((rows, width), BF16)
    id_like = pltpu.VMEM((picks, toks), jnp.int32)
    rw_like = pltpu.VMEM((picks, toks), F32)
    sems = pltpu.SemaphoreType.DMA
    return pl.pallas_call(
        functools.partial(kernel, slots, tile),
        out_shape=jax.ShapeDtypeStruct((toks, width), BF16),
        in_specs=[hbm] * 6,
        out_specs=vmem,
        scratch_shapes=[tok_like, id_like, rw_like,
                        pltpu.VMEM((2, toks, width), BF16), pltpu.VMEM((2, picks, toks), jnp.int32),
                        pltpu.VMEM((2, picks, toks), F32), near_like, pltpu.VMEM((2, mine, width), BF16),
                        all_like, all_like, near_like, pltpu.VMEM((2, mine, width), BF16),
                        pltpu.VMEM((2, toks, width), BF16), tok_like, pltpu.VMEM((toks, width), F32)]
        + [pltpu.VMEM((2 * half, width), BF16)] * 3
        + [pltpu.VMEM((mine, 2 * half), BF16)]
        + [sems((6,)), sems((3,)), sems((3,)), sems((chunks,)), sems((2, chunks)), sems((2,)), sems((2, 2)),
           sems((near,)), sems((near,)), sems((2, near, chunks)), sems((2, 2, chunks)),
           sems((near,)), sems((near,)), sems((2, 2, chunks)), sems((2, near, chunks)),
           sems((2, chunks)), sems((chunks,))],
        compiler_params=pltpu.CompilerParams(
            collective_id=0, has_side_effects=True, vmem_limit_bytes=60 * 1024 * 1024),
        cost_estimate=pl.CostEstimate(
            flops=12 * rows * half * width, bytes_accessed=6 * half * width + 4 * toks * width,
            transcendentals=2 * rows * half),
    )(tokens, expert_ids.T, route_weights.T, gate_weight, up_weight, down_weight)


def solution(mesh):
    in_specs = (
        P(("groups", "wide"), "narrow"),
        P(("groups", "wide"), None),
        P(("groups", "wide"), None),
        P("wide", "narrow", None),
        P("wide", "narrow", None),
        P("wide", "narrow", None),
    )
    out_specs = P(("groups", "wide"), "narrow")
    whole_rows = mesh.shape["narrow"] == 1 and mesh.shape["wide"] == 16
    return jax.shard_map(
        fused if whole_rows else per_device, mesh=mesh, in_specs=in_specs, out_specs=out_specs, check_vma=False
    )
```

```python
import functools

import jax
import jax.numpy as jnp
from jax import lax
from jax.experimental import pallas as pl
from jax.experimental.pallas import tpu as pltpu
from jax.sharding import PartitionSpec as P

F32 = jnp.float32
BF16 = jnp.bfloat16


def per_device(tokens, expert_ids, route_weights, gate_weight, up_weight, down_weight):
    tok_rows = tokens.shape[0]
    picks = expert_ids.shape[1]
    width_wide = lax.axis_size("wide")
    experts = width_wide // 2
    slots = 4 * tok_rows * picks // width_wide
    payload = lax.all_gather(tokens, "narrow", axis=1, tiled=True)
    feature_width = payload.shape[1]
    flat_ids = expert_ids.reshape(-1)
    flat_weights = route_weights.reshape(-1)
    onehot = (flat_ids[:, None] == jnp.arange(experts, dtype=jnp.int32)[None, :]).astype(jnp.int32)
    slot_rank = jnp.sum(jnp.cumsum(onehot, axis=0) * onehot, axis=1) - 1
    slot_place = flat_ids * slots + slot_rank
    token_source = jnp.arange(tok_rows * picks, dtype=jnp.int32) // picks
    slot_token = jnp.full((experts * slots,), tok_rows, jnp.int32).at[slot_place].set(token_source)
    padded = jnp.concatenate([payload, jnp.zeros((1, feature_width), payload.dtype)], axis=0)
    buffer = padded[slot_token].reshape(experts, slots, feature_width)
    outgoing = jnp.repeat(buffer, 2, axis=0)
    received = lax.all_to_all(outgoing, "wide", split_axis=0, concat_axis=0, tiled=True)
    model_width = received.shape[2]
    rows = received.reshape(width_wide * slots, model_width)
    gate = jnp.einsum("rd,hd->rh", rows, gate_weight[0], preferred_element_type=jnp.float32)
    up_part = jnp.einsum("rd,hd->rh", rows, up_weight[0], preferred_element_type=jnp.float32)
    hidden = (jax.nn.silu(gate) * up_part).astype(jnp.bfloat16)
    quarter_out = jnp.dot(hidden, down_weight[0], preferred_element_type=jnp.float32)
    quarter_blocks = quarter_out.reshape(width_wide, slots, model_width)
    returned = lax.all_to_all(quarter_blocks, "wide", split_axis=0, concat_axis=0, tiled=True)
    by_expert = jnp.sum(returned.reshape(experts, 2, slots, model_width), axis=1)
    pieces = by_expert[flat_ids, slot_rank]
    expert_total = lax.psum_scatter(pieces, "narrow", scatter_dimension=1, tiled=True)
    rounded = lax.optimization_barrier(expert_total.astype(jnp.bfloat16))
    pair_total = rounded.astype(jnp.float32) * flat_weights[:, None]
    column_width = pair_total.shape[1]
    mixed = jnp.sum(pair_total.reshape(tok_rows, picks, column_width), axis=1)
    return mixed.astype(jnp.bfloat16)


def flip(number, mask, bits):
    out = number
    for b in range(bits):
        if (mask >> b) & 1:
            bit = lax.rem(lax.div(number, 1 << b), 2)
            out = out + (1 - 2 * bit) * (1 << b)
    return out


def column(row):
    n = row.shape[1]
    same = lax.broadcasted_iota(jnp.int32, (n, n), 0) == lax.broadcasted_iota(jnp.int32, (n, n), 1)
    return jnp.sum(jnp.where(same, row, 0.0), axis=1, keepdims=True)


def one_hots(ids, experts, slots):
    toks = ids.shape[1]
    cols = len(experts) * slots
    id0 = column(ids[0:1, :].astype(F32))
    id1 = column(ids[1:2, :].astype(F32))
    col = lax.broadcasted_iota(jnp.int32, (toks, cols), 1)
    expert = jnp.zeros((toks, cols), F32)
    first = jnp.zeros((toks, cols), jnp.int32)
    for r, e in enumerate(experts):
        inside = (col >= r * slots) & (col < (r + 1) * slots)
        expert = jnp.where(inside, e.astype(F32), expert)
        first = jnp.where(inside, r * slots, first)
    pick0 = jnp.where(id0 == expert, 1.0, 0.0)
    pick1 = jnp.where(id1 == expert, 1.0, 0.0)
    named = pick0 + pick1
    before = jnp.where(lax.broadcasted_iota(jnp.int32, (toks, toks), 0)
                       > lax.broadcasted_iota(jnp.int32, (toks, toks), 1), 1.0, 0.0)
    rank = jnp.dot(before.astype(BF16), named.astype(BF16), preferred_element_type=F32)
    here = jnp.where(rank == (col - first).astype(F32), 1.0, 0.0)
    choose = jnp.transpose(here * named).astype(BF16)
    return choose, (here * pick0).astype(BF16), (here * pick1).astype(BF16)


def kernel(slots, tile, tok, ids, rw, gw, uw, dw, out,
           tokbuf, idbuf, rwbuf, fartok, farid, farrw, nearsend, relaysend, recvbuf, outbuf,
           nearret, farret, mixfar, mixback, nearsum, gubuf, dbuf, hid, kept, lent, lentback,
           local_sem, s_send, s_recv, x_send, x_recv, t_send, t_recv, m_send, m_recv, n_send, n_recv,
           l_send, l_recv, b_send, b_recv, f_send, f_recv, c_send, c_recv):
    near = 4
    half = gw.shape[1]
    width = tok.shape[1]
    chunks = width // tile
    mine = near * slots
    me = lax.axis_index("wide")
    chip = lax.div(me, 2)
    core = lax.rem(me, 2)
    z = lax.div(chip, 2)
    inner = lax.rem(z + 1, 4) >= 2
    outer = lax.rem(z + 1, 4) < 2
    slot = jnp.where(inner, 0, 1)
    sibling = 2 * chip + 1 - core
    partner = [flip(chip, r, 3) for r in range(near)]
    device = [2 * p + core for p in partner]
    across = [2 * flip(chip, 6, 3) + core, 2 * flip(chip, 4, 3) + core]
    relay_of_me = jnp.where(inner, across[0], across[1])

    def remote(src, dst, send, recv, to):
        return pltpu.make_async_remote_copy(src_ref=src, dst_ref=dst, send_sem=send, recv_sem=recv,
                                            device_id={"wide": to}, device_id_type=pl.DeviceIdType.MESH)

    barrier = pltpu.get_barrier_semaphore()
    for to in across + [sibling] + device[1:]:
        pl.semaphore_signal(barrier, inc=1, device_id={"wide": to}, device_id_type=pl.DeviceIdType.MESH)

    small = [pltpu.make_async_copy(src, dst, local_sem.at[1 + i])
             for i, (src, dst) in enumerate(((ids, idbuf), (rw, rwbuf), (tok, tokbuf)))]
    lanes = 128
    parts = half // lanes
    local = [pltpu.make_async_copy(src.at[0, pl.ds(i * lanes, lanes)], gubuf.at[pl.ds((2 * i + p) * lanes, lanes)],
                                   local_sem.at[4 + 2 * i + p])
             for i in range(parts) for p, src in enumerate((gw, uw))]
    local.append(pltpu.make_async_copy(dw.at[0], dbuf, local_sem.at[0]))
    for c in small + local:
        c.start()

    sizes = [mine, 2 * slots, 2 * slots]
    begins = [0, mine, mine + 2 * slots]
    span = [pl.ds(r * slots, slots) for r in range(2 * near)]
    cuts = [pl.ds(c * tile, tile) for c in range(chunks)]
    sides = range(2)

    def crossing(at):
        meta = [remote(ids, farid.at[at], m_send.at[0], m_recv.at[at, 0], relay_of_me),
                remote(rw, farrw.at[at], m_send.at[1], m_recv.at[at, 1], relay_of_me)]
        return meta, [remote(tok.at[:, cuts[c]], fartok.at[at, :, cuts[c]], t_send.at[c], t_recv.at[at, c],
                             relay_of_me) for c in range(chunks)]

    meta, over = crossing(slot)
    arriving = [crossing(g) for g in sides]
    direct = [remote(nearsend.at[span[r]], recvbuf.at[span[r]], n_send.at[r], n_recv.at[r], device[r])
              for r in range(1, near)]
    back = [remote(outbuf.at[span[r]], nearret.at[span[r]], b_send.at[r], b_recv.at[r], device[r])
            for r in range(1, near)]

    def block(g, i):
        return span[near + 2 * g + i]

    def landing(g, i):
        return pl.ds(2 * begins[1 + g] + i * slots, slots)

    share = [remote(recvbuf.at[pl.ds(2 * begins[g], sizes[g])], recvbuf.at[pl.ds(2 * begins[g] + sizes[g], sizes[g])],
                    s_send.at[g], s_recv.at[g], sibling) for g in range(3)]
    lend = [[remote(lent.at[pl.ds(begins[g], sizes[g]), cuts[c]], lentback.at[pl.ds(begins[g], sizes[g]), cuts[c]],
                    x_send.at[g, c], x_recv.at[g, c], sibling) for c in range(chunks)] for g in range(3)]

    relay = [[[remote(relaysend.at[g, span[r], cuts[c]], recvbuf.at[landing(g, r % 2), cuts[c]],
                      l_send.at[g, r, c], l_recv.at[g, r % 2, c], device[r]) for r in (2, 3, 1)]
              for c in range(chunks)] for g in sides]
    answer = [[[None] + [remote(outbuf.at[block(g, r % 2), cuts[c]], farret.at[g, span[r], cuts[c]],
                                f_send.at[g, r % 2, c], f_recv.at[g, r, c], device[r]) for r in range(1, near)]
               for c in range(chunks)] for g in sides]
    home = [[remote(mixfar.at[g, :, cuts[c]], mixback.at[:, cuts[c]], c_send.at[g, c], c_recv.at[c], across[g])
             for c in range(chunks)] for g in sides]

    pl.semaphore_wait(barrier, near + 2)

    @pl.when(inner)
    def _():
        for c in meta + over:
            c.start()

    for c in small:
        c.wait()
    choose, near0, near1 = one_hots(idbuf, partner, slots)
    for c in range(chunks):
        cut = slice(c * tile, (c + 1) * tile)
        picked = jnp.dot(choose, tokbuf[:, cut], preferred_element_type=F32).astype(BF16)
        nearsend[:, cut] = picked
        recvbuf[0:slots, cut] = picked[0:slots]
    for c in direct:
        c.start()

    @pl.when(outer)
    def _():
        for c in meta + over:
            c.start()

    @pl.when(inner)
    def _():
        for g in sides:
            for c in arriving[g][0]:
                c.wait_recv()
            choose, unused0, unused1 = one_hots(farid.at[g], partner, slots)
            for c in range(chunks):
                cut = slice(c * tile, (c + 1) * tile)
                arriving[g][1][c].wait_recv()
                picked = jnp.dot(choose, fartok[g, :, cut], preferred_element_type=F32).astype(BF16)
                relaysend[g, :, cut] = picked
                low = 2 * begins[1 + g]
                recvbuf[low:low + slots, cut] = picked[0:slots]
                for copy in relay[g][c]:
                    copy.start()

    for c in local:
        c.wait()

    def experts(g, answers):
        size, base = sizes[g], 2 * begins[g]
        share[g].start()
        share[g].wait_recv()

        @pl.loop(0, parts)
        def _(i):
            at = pl.ds(pl.multiple_of(i * 2 * lanes, 2 * lanes), 2 * lanes)
            both = lax.dot_general(recvbuf[base:base + 2 * size, :], gubuf[at, :], (((1,), (1,)), ((), ())),
                                   preferred_element_type=F32)
            gate, up = both[:, 0:lanes], both[:, lanes:2 * lanes]
            hid[0:2 * size, pl.ds(pl.multiple_of(i * lanes, lanes), lanes)] = (
                gate / (1.0 + jnp.exp(-gate)) * up).astype(BF16)

        low = begins[g]
        for c in range(chunks):
            cut = slice(c * tile, (c + 1) * tile)
            part = jnp.dot(hid[0:2 * size, :], dbuf[:, cut], preferred_element_type=F32)
            kept[0:size, cut] = part[0:size]
            lent[low:low + size, cut] = part[size:2 * size].astype(BF16)
            lend[g][c].start()
        for c in range(chunks):
            cut = slice(c * tile, (c + 1) * tile)
            lend[g][c].wait_recv()
            part = (kept[0:size, cut] + lentback[low:low + size, cut].astype(F32)).astype(BF16)
            outbuf[low:low + size, cut] = part
            answers(c, cut, part)

    def near_answers(c, cut, part):
        nearret[0:slots, cut] = part[0:slots]

    for c in direct:
        c.wait_recv()
    experts(0, near_answers)
    for c in back:
        c.start()

    for g in sides:
        @pl.when(outer)
        def _():
            for c in range(chunks):
                relay[g][c][0].wait_recv()

        for c in range(chunks):
            relay[g][c][2].wait_recv()

        def far_answers(c, cut, part):
            farret[g, 0:slots, cut] = part[0:slots]

            @pl.when(inner)
            def _():
                answer[g][c][1].start()

            @pl.when(outer)
            def _():
                answer[g][c][2].start()
                answer[g][c][3].start()

        experts(1 + g, far_answers)

    @pl.when(inner)
    def _():
        for g in sides:
            unused, far0, far1 = one_hots(farid.at[g], partner, slots)
            w0, w1 = column(farrw[g, 0:1, :]), column(farrw[g, 1:2, :])
            for c in range(chunks):
                cut = slice(c * tile, (c + 1) * tile)
                for r in range(1, near):
                    answer[g][c][r].wait_recv()
                part = farret[g, :, cut]
                mixfar[g, :, cut] = (w0 * jnp.dot(far0, part, preferred_element_type=F32)
                                     + w1 * jnp.dot(far1, part, preferred_element_type=F32)).astype(BF16)
                home[g][c].start()

    w0, w1 = column(rwbuf[0:1, :]), column(rwbuf[1:2, :])
    for c in back:
        c.wait_recv()
    for c in range(chunks):
        cut = slice(c * tile, (c + 1) * tile)
        part = nearret[:, cut]
        nearsum[:, cut] = (w0 * jnp.dot(near0, part, preferred_element_type=F32)
                           + w1 * jnp.dot(near1, part, preferred_element_type=F32))
    for c in range(chunks):
        cut = slice(c * tile, (c + 1) * tile)
        home[0][c].wait_recv()
        out[:, cut] = (nearsum[:, cut] + mixback[:, cut].astype(F32)).astype(BF16)

    for c in meta + over + direct + back + share + lend[0] + lend[1] + lend[2]:
        c.wait_send()

    @pl.when(inner)
    def _():
        for g in sides:
            for c in range(chunks):
                for copy in relay[g][c]:
                    copy.wait_send()
                answer[g][c][1].wait_send()
                home[g][c].wait_send()

    @pl.when(outer)
    def _():
        for g in sides:
            for c in range(chunks):
                answer[g][c][2].wait_send()
                answer[g][c][3].wait_send()


def fused(tokens, expert_ids, route_weights, gate_weight, up_weight, down_weight):
    toks, width = tokens.shape
    picks = expert_ids.shape[1]
    wide = lax.axis_size("wide")
    chips = wide // 2
    near = chips // 2
    slots = 4 * toks * picks // wide
    half = gate_weight.shape[1]
    rows = chips * slots
    mine = near * slots
    tile = 512
    chunks = width // tile
    vmem = pl.BlockSpec(memory_space=pltpu.VMEM)
    hbm = pl.BlockSpec(memory_space=pl.ANY)
    tok_like = pltpu.VMEM((toks, width), BF16)
    near_like = pltpu.VMEM((mine, width), BF16)
    all_like = pltpu.VMEM((rows, width), BF16)
    id_like = pltpu.VMEM((picks, toks), jnp.int32)
    rw_like = pltpu.VMEM((picks, toks), F32)
    sems = pltpu.SemaphoreType.DMA
    return pl.pallas_call(
        functools.partial(kernel, slots, tile),
        out_shape=jax.ShapeDtypeStruct((toks, width), BF16),
        in_specs=[hbm] * 6,
        out_specs=vmem,
        scratch_shapes=[tok_like, id_like, rw_like,
                        pltpu.VMEM((2, toks, width), BF16), pltpu.VMEM((2, picks, toks), jnp.int32),
                        pltpu.VMEM((2, picks, toks), F32), near_like, pltpu.VMEM((2, mine, width), BF16),
                        pltpu.VMEM((2 * rows, width), BF16), all_like, near_like, pltpu.VMEM((2, mine, width), BF16),
                        pltpu.VMEM((2, toks, width), BF16), tok_like, pltpu.VMEM((toks, width), F32)]
        + [pltpu.VMEM((2 * half, width), BF16), pltpu.VMEM((half, width), BF16),
           pltpu.VMEM((2 * mine, half), BF16), pltpu.VMEM((mine, width), F32), all_like, all_like]
        + [sems((4 + 2 * (half // 128),)), sems((3,)), sems((3,)), sems((3, chunks)), sems((3, chunks)), sems((chunks,)), sems((2, chunks)), sems((2,)), sems((2, 2)),
           sems((near,)), sems((near,)), sems((2, near, chunks)), sems((2, 2, chunks)),
           sems((near,)), sems((near,)), sems((2, 2, chunks)), sems((2, near, chunks)),
           sems((2, chunks)), sems((chunks,))],
        compiler_params=pltpu.CompilerParams(
            collective_id=0, has_side_effects=True, vmem_limit_bytes=60 * 1024 * 1024),
        cost_estimate=pl.CostEstimate(
            flops=12 * rows * half * width, bytes_accessed=6 * half * width + 4 * toks * width,
            transcendentals=2 * rows * half),
    )(tokens, expert_ids.T, route_weights.T, gate_weight, up_weight, down_weight)


def solution(mesh):
    in_specs = (
        P(("groups", "wide"), "narrow"),
        P(("groups", "wide"), None),
        P(("groups", "wide"), None),
        P("wide", "narrow", None),
        P("wide", "narrow", None),
        P("wide", "narrow", None),
    )
    out_specs = P(("groups", "wide"), "narrow")
    whole_rows = mesh.shape["narrow"] == 1 and mesh.shape["wide"] == 16
    return jax.shard_map(
        fused if whole_rows else per_device, mesh=mesh, in_specs=in_specs, out_specs=out_specs, check_vma=False
    )
```

```python
import functools

import jax
import jax.numpy as jnp
from jax import lax
from jax.experimental import pallas as pl
from jax.experimental.pallas import tpu as pltpu
from jax.sharding import PartitionSpec as P

F32 = jnp.float32
BF16 = jnp.bfloat16


def per_device(tokens, expert_ids, route_weights, gate_weight, up_weight, down_weight):
    tok_rows = tokens.shape[0]
    picks = expert_ids.shape[1]
    width_wide = lax.axis_size("wide")
    experts = width_wide // 2
    slots = 4 * tok_rows * picks // width_wide
    payload = lax.all_gather(tokens, "narrow", axis=1, tiled=True)
    feature_width = payload.shape[1]
    flat_ids = expert_ids.reshape(-1)
    flat_weights = route_weights.reshape(-1)
    onehot = (flat_ids[:, None] == jnp.arange(experts, dtype=jnp.int32)[None, :]).astype(jnp.int32)
    slot_rank = jnp.sum(jnp.cumsum(onehot, axis=0) * onehot, axis=1) - 1
    slot_place = flat_ids * slots + slot_rank
    token_source = jnp.arange(tok_rows * picks, dtype=jnp.int32) // picks
    slot_token = jnp.full((experts * slots,), tok_rows, jnp.int32).at[slot_place].set(token_source)
    padded = jnp.concatenate([payload, jnp.zeros((1, feature_width), payload.dtype)], axis=0)
    buffer = padded[slot_token].reshape(experts, slots, feature_width)
    outgoing = jnp.repeat(buffer, 2, axis=0)
    received = lax.all_to_all(outgoing, "wide", split_axis=0, concat_axis=0, tiled=True)
    model_width = received.shape[2]
    rows = received.reshape(width_wide * slots, model_width)
    gate = jnp.einsum("rd,hd->rh", rows, gate_weight[0], preferred_element_type=jnp.float32)
    up_part = jnp.einsum("rd,hd->rh", rows, up_weight[0], preferred_element_type=jnp.float32)
    hidden = (jax.nn.silu(gate) * up_part).astype(jnp.bfloat16)
    quarter_out = jnp.dot(hidden, down_weight[0], preferred_element_type=jnp.float32)
    quarter_blocks = quarter_out.reshape(width_wide, slots, model_width)
    returned = lax.all_to_all(quarter_blocks, "wide", split_axis=0, concat_axis=0, tiled=True)
    by_expert = jnp.sum(returned.reshape(experts, 2, slots, model_width), axis=1)
    pieces = by_expert[flat_ids, slot_rank]
    expert_total = lax.psum_scatter(pieces, "narrow", scatter_dimension=1, tiled=True)
    rounded = lax.optimization_barrier(expert_total.astype(jnp.bfloat16))
    pair_total = rounded.astype(jnp.float32) * flat_weights[:, None]
    column_width = pair_total.shape[1]
    mixed = jnp.sum(pair_total.reshape(tok_rows, picks, column_width), axis=1)
    return mixed.astype(jnp.bfloat16)


def flip(number, mask, bits):
    out = number
    for b in range(bits):
        if (mask >> b) & 1:
            bit = lax.rem(lax.div(number, 1 << b), 2)
            out = out + (1 - 2 * bit) * (1 << b)
    return out


def column(row):
    n = row.shape[1]
    same = lax.broadcasted_iota(jnp.int32, (n, n), 0) == lax.broadcasted_iota(jnp.int32, (n, n), 1)
    return jnp.sum(jnp.where(same, row, 0.0), axis=1, keepdims=True)


def one_hots(ids, experts, slots):
    toks = ids.shape[1]
    cols = len(experts) * slots
    id0 = column(ids[0:1, :].astype(F32))
    id1 = column(ids[1:2, :].astype(F32))
    col = lax.broadcasted_iota(jnp.int32, (toks, cols), 1)
    expert = jnp.zeros((toks, cols), F32)
    first = jnp.zeros((toks, cols), jnp.int32)
    for r, e in enumerate(experts):
        inside = (col >= r * slots) & (col < (r + 1) * slots)
        expert = jnp.where(inside, e.astype(F32), expert)
        first = jnp.where(inside, r * slots, first)
    pick0 = jnp.where(id0 == expert, 1.0, 0.0)
    pick1 = jnp.where(id1 == expert, 1.0, 0.0)
    named = pick0 + pick1
    before = jnp.where(lax.broadcasted_iota(jnp.int32, (toks, toks), 0)
                       > lax.broadcasted_iota(jnp.int32, (toks, toks), 1), 1.0, 0.0)
    rank = jnp.dot(before.astype(BF16), named.astype(BF16), preferred_element_type=F32)
    here = jnp.where(rank == (col - first).astype(F32), 1.0, 0.0)
    choose = jnp.transpose(here * named).astype(BF16)
    return choose, (here * pick0).astype(BF16), (here * pick1).astype(BF16)


def kernel(slots, tile, tok, ids, rw, gw, uw, dw, out,
           tokbuf, idbuf, rwbuf, fartok, farid, farrw, nearsend, relaysend, recvbuf, outbuf,
           nearret, farret, mixfar, mixback, nearsum, gbuf, ubuf, dbuf, hid, turned,
           local_sem, w_send, w_recv, t_send, t_recv, m_send, m_recv, n_send, n_recv,
           l_send, l_recv, b_send, b_recv, f_send, f_recv, c_send, c_recv):
    near = 4
    half = gw.shape[1]
    width = tok.shape[1]
    chunks = width // tile
    mine = near * slots
    me = lax.axis_index("wide")
    chip = lax.div(me, 2)
    core = lax.rem(me, 2)
    z = lax.div(chip, 2)
    inner = lax.rem(z + 1, 4) >= 2
    outer = lax.rem(z + 1, 4) < 2
    slot = jnp.where(inner, 0, 1)
    sibling = 2 * chip + 1 - core
    partner = [flip(chip, r, 3) for r in range(near)]
    device = [2 * p + core for p in partner]
    across = [2 * flip(chip, 6, 3) + core, 2 * flip(chip, 4, 3) + core]
    relay_of_me = jnp.where(inner, across[0], across[1])

    def remote(src, dst, send, recv, to):
        return pltpu.make_async_remote_copy(src_ref=src, dst_ref=dst, send_sem=send, recv_sem=recv,
                                            device_id={"wide": to}, device_id_type=pl.DeviceIdType.MESH)

    barrier = pltpu.get_barrier_semaphore()
    for to in across + [sibling] + device[1:]:
        pl.semaphore_signal(barrier, inc=1, device_id={"wide": to}, device_id_type=pl.DeviceIdType.MESH)

    pairs = ((gw, gbuf), (uw, ubuf), (dw, dbuf))
    small = [pltpu.make_async_copy(src, dst, local_sem.at[3 + i])
             for i, (src, dst) in enumerate(((ids, idbuf), (rw, rwbuf), (tok, tokbuf)))]
    local = [pltpu.make_async_copy(src.at[0], dst.at[pl.ds(0, half)], local_sem.at[i])
             for i, (src, dst) in enumerate(pairs)]
    for c in small + local:
        c.start()

    span = [pl.ds(r * slots, slots) for r in range(2 * near)]
    cuts = [pl.ds(c * tile, tile) for c in range(chunks)]
    sides = range(2)

    def crossing(at):
        meta = [remote(ids, farid.at[at], m_send.at[0], m_recv.at[at, 0], relay_of_me),
                remote(rw, farrw.at[at], m_send.at[1], m_recv.at[at, 1], relay_of_me)]
        return meta, [remote(tok.at[:, cuts[c]], fartok.at[at, :, cuts[c]], t_send.at[c], t_recv.at[at, c],
                             relay_of_me) for c in range(chunks)]

    meta, over = crossing(slot)
    arriving = [crossing(g) for g in sides]
    swap = [remote(src.at[0], dst.at[pl.ds(half, half)], w_send.at[i], w_recv.at[i], sibling)
            for i, (src, dst) in enumerate(pairs)]
    direct = [remote(nearsend.at[span[r]], recvbuf.at[span[r]], n_send.at[r], n_recv.at[r], device[r])
              for r in range(1, near)]
    back = [remote(outbuf.at[span[r]], nearret.at[span[r]], b_send.at[r], b_recv.at[r], device[r])
            for r in range(1, near)]

    def block(g, i):
        return span[near + 2 * g + i]

    relay = [[[remote(relaysend.at[g, span[r], cuts[c]], recvbuf.at[block(g, r % 2), cuts[c]],
                      l_send.at[g, r, c], l_recv.at[g, r % 2, c], device[r]) for r in (2, 3, 1)]
              for c in range(chunks)] for g in sides]
    answer = [[[None] + [remote(outbuf.at[block(g, r % 2), cuts[c]], farret.at[g, span[r], cuts[c]],
                                f_send.at[g, r % 2, c], f_recv.at[g, r, c], device[r]) for r in range(1, near)]
               for c in range(chunks)] for g in sides]
    home = [[remote(mixfar.at[g, :, cuts[c]], mixback.at[:, cuts[c]], c_send.at[g, c], c_recv.at[c], across[g])
             for c in range(chunks)] for g in sides]

    pl.semaphore_wait(barrier, near + 2)

    @pl.when(inner)
    def _():
        for c in meta + over:
            c.start()

    for c in small:
        c.wait()
    choose, near0, near1 = one_hots(idbuf, partner, slots)
    for c in range(chunks):
        cut = slice(c * tile, (c + 1) * tile)
        picked = jnp.dot(choose, tokbuf[:, cut], preferred_element_type=F32).astype(BF16)
        nearsend[:, cut] = picked
        recvbuf[0:slots, cut] = picked[0:slots]
    for c in direct:
        c.start()

    @pl.when(outer)
    def _():
        for c in meta + over:
            c.start()

    for c in swap:
        c.start()

    @pl.when(inner)
    def _():
        for g in sides:
            for c in arriving[g][0]:
                c.wait_recv()
            choose, unused0, unused1 = one_hots(farid.at[g], partner, slots)
            for c in range(chunks):
                cut = slice(c * tile, (c + 1) * tile)
                arriving[g][1][c].wait_recv()
                picked = jnp.dot(choose, fartok[g, :, cut], preferred_element_type=F32).astype(BF16)
                relaysend[g, :, cut] = picked
                low = mine + 2 * g * slots
                recvbuf[low:low + slots, cut] = picked[0:slots]
                for copy in relay[g][c]:
                    copy.start()

    for c in local:
        c.wait()
    for c in swap:
        c.wait_recv()

    hid_tile = 256

    def turn(base, rows, c):
        cut = slice(c * tile, (c + 1) * tile)
        turned[cut, 0:rows] = jnp.transpose(recvbuf[base:base + rows, cut])

    def into_hidden(rows):
        @pl.loop(0, 2 * half // hid_tile)
        def _(i):
            at = pl.ds(pl.multiple_of(i * hid_tile, hid_tile), hid_tile)
            x = turned[:, 0:rows]
            gate = jnp.dot(gbuf[at, :], x, preferred_element_type=F32)
            up = jnp.dot(ubuf[at, :], x, preferred_element_type=F32)
            hid[0:rows, at] = jnp.transpose(gate / (1.0 + jnp.exp(-gate)) * up).astype(BF16)

    for c in direct:
        c.wait_recv()
    for c in range(chunks):
        turn(0, mine, c)
    into_hidden(mine)
    for c in range(chunks):
        cut = slice(c * tile, (c + 1) * tile)
        part = jnp.dot(hid[...], dbuf[:, cut], preferred_element_type=F32).astype(BF16)
        outbuf[0:mine, cut] = part
        nearret[0:slots, cut] = part[0:slots]
    for c in back:
        c.start()

    for g in sides:
        low = mine + 2 * g * slots

        for c in range(chunks):
            @pl.when(outer)
            def _():
                relay[g][c][0].wait_recv()

            relay[g][c][2].wait_recv()
            turn(low, 2 * slots, c)
        into_hidden(2 * slots)
        for c in range(chunks):
            cut = slice(c * tile, (c + 1) * tile)
            part = jnp.dot(hid[0:2 * slots, :], dbuf[:, cut], preferred_element_type=F32).astype(BF16)
            outbuf[low:low + 2 * slots, cut] = part
            farret[g, 0:slots, cut] = part[0:slots]

            @pl.when(inner)
            def _():
                answer[g][c][1].start()

            @pl.when(outer)
            def _():
                answer[g][c][2].start()
                answer[g][c][3].start()

    @pl.when(inner)
    def _():
        for g in sides:
            unused, far0, far1 = one_hots(farid.at[g], partner, slots)
            w0, w1 = column(farrw[g, 0:1, :]), column(farrw[g, 1:2, :])
            for c in range(chunks):
                cut = slice(c * tile, (c + 1) * tile)
                for r in range(1, near):
                    answer[g][c][r].wait_recv()
                part = farret[g, :, cut]
                mixfar[g, :, cut] = (w0 * jnp.dot(far0, part, preferred_element_type=F32)
                                     + w1 * jnp.dot(far1, part, preferred_element_type=F32)).astype(BF16)
                home[g][c].start()

    w0, w1 = column(rwbuf[0:1, :]), column(rwbuf[1:2, :])
    for c in back:
        c.wait_recv()
    for c in range(chunks):
        cut = slice(c * tile, (c + 1) * tile)
        part = nearret[:, cut]
        nearsum[:, cut] = (w0 * jnp.dot(near0, part, preferred_element_type=F32)
                           + w1 * jnp.dot(near1, part, preferred_element_type=F32))
    for c in range(chunks):
        cut = slice(c * tile, (c + 1) * tile)
        home[0][c].wait_recv()
        out[:, cut] = (nearsum[:, cut] + mixback[:, cut].astype(F32)).astype(BF16)

    for c in meta + over + swap + direct + back:
        c.wait_send()

    @pl.when(inner)
    def _():
        for g in sides:
            for c in range(chunks):
                for copy in relay[g][c]:
                    copy.wait_send()
                answer[g][c][1].wait_send()
                home[g][c].wait_send()

    @pl.when(outer)
    def _():
        for g in sides:
            for c in range(chunks):
                answer[g][c][2].wait_send()
                answer[g][c][3].wait_send()


def fused(tokens, expert_ids, route_weights, gate_weight, up_weight, down_weight):
    toks, width = tokens.shape
    picks = expert_ids.shape[1]
    wide = lax.axis_size("wide")
    chips = wide // 2
    near = chips // 2
    slots = 4 * toks * picks // wide
    half = gate_weight.shape[1]
    rows = chips * slots
    mine = near * slots
    tile = 512
    chunks = width // tile
    vmem = pl.BlockSpec(memory_space=pltpu.VMEM)
    hbm = pl.BlockSpec(memory_space=pl.ANY)
    tok_like = pltpu.VMEM((toks, width), BF16)
    near_like = pltpu.VMEM((mine, width), BF16)
    all_like = pltpu.VMEM((rows, width), BF16)
    id_like = pltpu.VMEM((picks, toks), jnp.int32)
    rw_like = pltpu.VMEM((picks, toks), F32)
    sems = pltpu.SemaphoreType.DMA
    return pl.pallas_call(
        functools.partial(kernel, slots, tile),
        out_shape=jax.ShapeDtypeStruct((toks, width), BF16),
        in_specs=[hbm] * 6,
        out_specs=vmem,
        scratch_shapes=[tok_like, id_like, rw_like,
                        pltpu.VMEM((2, toks, width), BF16), pltpu.VMEM((2, picks, toks), jnp.int32),
                        pltpu.VMEM((2, picks, toks), F32), near_like, pltpu.VMEM((2, mine, width), BF16),
                        all_like, all_like, near_like, pltpu.VMEM((2, mine, width), BF16),
                        pltpu.VMEM((2, toks, width), BF16), tok_like, pltpu.VMEM((toks, width), F32)]
        + [pltpu.VMEM((2 * half, width), BF16)] * 3
        + [pltpu.VMEM((mine, 2 * half), BF16), pltpu.VMEM((width, mine), BF16)]
        + [sems((6,)), sems((3,)), sems((3,)), sems((chunks,)), sems((2, chunks)), sems((2,)), sems((2, 2)),
           sems((near,)), sems((near,)), sems((2, near, chunks)), sems((2, 2, chunks)),
           sems((near,)), sems((near,)), sems((2, 2, chunks)), sems((2, near, chunks)),
           sems((2, chunks)), sems((chunks,))],
        compiler_params=pltpu.CompilerParams(
            collective_id=0, has_side_effects=True, vmem_limit_bytes=60 * 1024 * 1024),
        cost_estimate=pl.CostEstimate(
            flops=12 * rows * half * width, bytes_accessed=6 * half * width + 4 * toks * width,
            transcendentals=2 * rows * half),
    )(tokens, expert_ids.T, route_weights.T, gate_weight, up_weight, down_weight)


def solution(mesh):
    in_specs = (
        P(("groups", "wide"), "narrow"),
        P(("groups", "wide"), None),
        P(("groups", "wide"), None),
        P("wide", "narrow", None),
        P("wide", "narrow", None),
        P("wide", "narrow", None),
    )
    out_specs = P(("groups", "wide"), "narrow")
    whole_rows = mesh.shape["narrow"] == 1 and mesh.shape["wide"] == 16
    return jax.shard_map(
        fused if whole_rows else per_device, mesh=mesh, in_specs=in_specs, out_specs=out_specs, check_vma=False
    )
```

```python
import functools

import jax
import jax.numpy as jnp
from jax import lax
from jax.experimental import pallas as pl
from jax.experimental.pallas import tpu as pltpu
from jax.sharding import PartitionSpec as P

F32 = jnp.float32
BF16 = jnp.bfloat16


def per_device(tokens, expert_ids, route_weights, gate_weight, up_weight, down_weight):
    tok_rows = tokens.shape[0]
    picks = expert_ids.shape[1]
    width_wide = lax.axis_size("wide")
    experts = width_wide // 2
    slots = 4 * tok_rows * picks // width_wide
    payload = lax.all_gather(tokens, "narrow", axis=1, tiled=True)
    feature_width = payload.shape[1]
    flat_ids = expert_ids.reshape(-1)
    flat_weights = route_weights.reshape(-1)
    onehot = (flat_ids[:, None] == jnp.arange(experts, dtype=jnp.int32)[None, :]).astype(jnp.int32)
    slot_rank = jnp.sum(jnp.cumsum(onehot, axis=0) * onehot, axis=1) - 1
    slot_place = flat_ids * slots + slot_rank
    token_source = jnp.arange(tok_rows * picks, dtype=jnp.int32) // picks
    slot_token = jnp.full((experts * slots,), tok_rows, jnp.int32).at[slot_place].set(token_source)
    padded = jnp.concatenate([payload, jnp.zeros((1, feature_width), payload.dtype)], axis=0)
    buffer = padded[slot_token].reshape(experts, slots, feature_width)
    outgoing = jnp.repeat(buffer, 2, axis=0)
    received = lax.all_to_all(outgoing, "wide", split_axis=0, concat_axis=0, tiled=True)
    model_width = received.shape[2]
    rows = received.reshape(width_wide * slots, model_width)
    gate = jnp.einsum("rd,hd->rh", rows, gate_weight[0], preferred_element_type=jnp.float32)
    up_part = jnp.einsum("rd,hd->rh", rows, up_weight[0], preferred_element_type=jnp.float32)
    hidden = (jax.nn.silu(gate) * up_part).astype(jnp.bfloat16)
    quarter_out = jnp.dot(hidden, down_weight[0], preferred_element_type=jnp.float32)
    quarter_blocks = quarter_out.reshape(width_wide, slots, model_width)
    returned = lax.all_to_all(quarter_blocks, "wide", split_axis=0, concat_axis=0, tiled=True)
    by_expert = jnp.sum(returned.reshape(experts, 2, slots, model_width), axis=1)
    pieces = by_expert[flat_ids, slot_rank]
    expert_total = lax.psum_scatter(pieces, "narrow", scatter_dimension=1, tiled=True)
    rounded = lax.optimization_barrier(expert_total.astype(jnp.bfloat16))
    pair_total = rounded.astype(jnp.float32) * flat_weights[:, None]
    column_width = pair_total.shape[1]
    mixed = jnp.sum(pair_total.reshape(tok_rows, picks, column_width), axis=1)
    return mixed.astype(jnp.bfloat16)


def flip(number, mask, bits):
    out = number
    for b in range(bits):
        if (mask >> b) & 1:
            bit = lax.rem(lax.div(number, 1 << b), 2)
            out = out + (1 - 2 * bit) * (1 << b)
    return out


def column(row):
    n = row.shape[1]
    same = lax.broadcasted_iota(jnp.int32, (n, n), 0) == lax.broadcasted_iota(jnp.int32, (n, n), 1)
    return jnp.sum(jnp.where(same, row, 0.0), axis=1, keepdims=True)


def one_hots(ids, experts, slots):
    toks = ids.shape[1]
    cols = len(experts) * slots
    id0 = column(ids[0:1, :].astype(F32))
    id1 = column(ids[1:2, :].astype(F32))
    col = lax.broadcasted_iota(jnp.int32, (toks, cols), 1)
    expert = jnp.zeros((toks, cols), F32)
    first = jnp.zeros((toks, cols), jnp.int32)
    for r, e in enumerate(experts):
        inside = (col >= r * slots) & (col < (r + 1) * slots)
        expert = jnp.where(inside, e.astype(F32), expert)
        first = jnp.where(inside, r * slots, first)
    pick0 = jnp.where(id0 == expert, 1.0, 0.0)
    pick1 = jnp.where(id1 == expert, 1.0, 0.0)
    named = pick0 + pick1
    before = jnp.where(lax.broadcasted_iota(jnp.int32, (toks, toks), 0)
                       > lax.broadcasted_iota(jnp.int32, (toks, toks), 1), 1.0, 0.0)
    rank = jnp.dot(before.astype(BF16), named.astype(BF16), preferred_element_type=F32)
    here = jnp.where(rank == (col - first).astype(F32), 1.0, 0.0)
    choose = jnp.transpose(here * named).astype(BF16)
    return choose, (here * pick0).astype(BF16), (here * pick1).astype(BF16)


def kernel(slots, tile, tok, ids, rw, gw, uw, dw, out,
           tokbuf, idbuf, rwbuf, fartok, farid, farrw, nearsend, relaysend, recvbuf, outbuf,
           nearret, farret, mixfar, mixback, nearsum, gbuf, ubuf, dbuf, hid,
           local_sem, w_send, w_recv, t_send, t_recv, m_send, m_recv, n_send, n_recv,
           l_send, l_recv, b_send, b_recv, f_send, f_recv, c_send, c_recv):
    near = 4
    half = gw.shape[1]
    width = tok.shape[1]
    chunks = width // tile
    mine = near * slots
    me = lax.axis_index("wide")
    chip = lax.div(me, 2)
    core = lax.rem(me, 2)
    z = lax.div(chip, 2)
    inner = lax.rem(z + 1, 4) >= 2
    outer = lax.rem(z + 1, 4) < 2
    slot = jnp.where(inner, 0, 1)
    sibling = 2 * chip + 1 - core
    partner = [flip(chip, r, 3) for r in range(near)]
    device = [2 * p + core for p in partner]
    across = [2 * flip(chip, 6, 3) + core, 2 * flip(chip, 4, 3) + core]
    relay_of_me = jnp.where(inner, across[0], across[1])

    def remote(src, dst, send, recv, to):
        return pltpu.make_async_remote_copy(src_ref=src, dst_ref=dst, send_sem=send, recv_sem=recv,
                                            device_id={"wide": to}, device_id_type=pl.DeviceIdType.MESH)

    barrier = pltpu.get_barrier_semaphore()
    for to in across + [sibling] + device[1:]:
        pl.semaphore_signal(barrier, inc=1, device_id={"wide": to}, device_id_type=pl.DeviceIdType.MESH)

    pairs = ((gw, gbuf), (uw, ubuf), (dw, dbuf))
    small = [pltpu.make_async_copy(src, dst, local_sem.at[3 + i])
             for i, (src, dst) in enumerate(((ids, idbuf), (rw, rwbuf), (tok, tokbuf)))]
    local = [pltpu.make_async_copy(src.at[0], dst.at[pl.ds(0, half)], local_sem.at[i])
             for i, (src, dst) in enumerate(pairs)]
    for c in small + local:
        c.start()

    span = [pl.ds(r * slots, slots) for r in range(2 * near)]
    cuts = [pl.ds(c * tile, tile) for c in range(chunks)]
    sides = range(2)

    def crossing(at):
        meta = [remote(ids, farid.at[at], m_send.at[0], m_recv.at[at, 0], relay_of_me),
                remote(rw, farrw.at[at], m_send.at[1], m_recv.at[at, 1], relay_of_me)]
        return meta, [remote(tok.at[:, cuts[c]], fartok.at[at, :, cuts[c]], t_send.at[c], t_recv.at[at, c],
                             relay_of_me) for c in range(chunks)]

    meta, over = crossing(slot)
    arriving = [crossing(g) for g in sides]
    swap = [remote(src.at[0], dst.at[pl.ds(half, half)], w_send.at[i], w_recv.at[i], sibling)
            for i, (src, dst) in enumerate(pairs)]
    direct = [remote(nearsend.at[span[r]], recvbuf.at[span[r]], n_send.at[r], n_recv.at[r], device[r])
              for r in range(1, near)]
    back = [remote(outbuf.at[span[r]], nearret.at[span[r]], b_send.at[r], b_recv.at[r], device[r])
            for r in range(1, near)]

    def block(g, i):
        return span[near + 2 * g + i]

    relay = [[[remote(relaysend.at[g, span[r], cuts[c]], recvbuf.at[block(g, r % 2), cuts[c]],
                      l_send.at[g, r, c], l_recv.at[g, r % 2, c], device[r]) for r in (2, 3, 1)]
              for c in range(chunks)] for g in sides]
    answer = [[[None] + [remote(outbuf.at[block(g, r % 2), cuts[c]], farret.at[g, span[r], cuts[c]],
                                f_send.at[g, r % 2, c], f_recv.at[g, r, c], device[r]) for r in range(1, near)]
               for c in range(chunks)] for g in sides]
    home = [[remote(mixfar.at[g, :, cuts[c]], mixback.at[:, cuts[c]], c_send.at[g, c], c_recv.at[c], across[g])
             for c in range(chunks)] for g in sides]

    pl.semaphore_wait(barrier, near + 2)

    @pl.when(inner)
    def _():
        for c in meta + over:
            c.start()

    for c in small:
        c.wait()
    choose, near0, near1 = one_hots(idbuf, partner, slots)
    for c in range(chunks):
        cut = slice(c * tile, (c + 1) * tile)
        picked = jnp.dot(choose, tokbuf[:, cut], preferred_element_type=F32).astype(BF16)
        nearsend[:, cut] = picked
        recvbuf[0:slots, cut] = picked[0:slots]
    for c in direct:
        c.start()

    @pl.when(outer)
    def _():
        for c in meta + over:
            c.start()

    for c in swap:
        c.start()

    @pl.when(inner)
    def _():
        for g in sides:
            for c in arriving[g][0]:
                c.wait_recv()
            choose, unused0, unused1 = one_hots(farid.at[g], partner, slots)
            for c in range(chunks):
                cut = slice(c * tile, (c + 1) * tile)
                arriving[g][1][c].wait_recv()
                picked = jnp.dot(choose, fartok[g, :, cut], preferred_element_type=F32).astype(BF16)
                relaysend[g, :, cut] = picked
                low = mine + 2 * g * slots
                recvbuf[low:low + slots, cut] = picked[0:slots]
                for copy in relay[g][c]:
                    copy.start()

    for c in local:
        c.wait()
    for c in swap:
        c.wait_recv()

    hid_tile = 256

    def into_hidden(base, rows):
        @pl.loop(0, 2 * half // hid_tile)
        def _(i):
            at = pl.ds(pl.multiple_of(i * hid_tile, hid_tile), hid_tile)
            x = recvbuf[base:base + rows, :]
            dims = (((1,), (1,)), ((), ()))
            gate = lax.dot_general(x, gbuf[at, :], dims, preferred_element_type=F32)
            up = lax.dot_general(x, ubuf[at, :], dims, preferred_element_type=F32)
            hid[0:rows, at] = (gate / (1.0 + jnp.exp(-gate)) * up).astype(BF16)

    def near_group():
        for c in direct:
            c.wait_recv()
        into_hidden(0, mine)
        for c in range(chunks):
            cut = slice(c * tile, (c + 1) * tile)
            part = jnp.dot(hid[...], dbuf[:, cut], preferred_element_type=F32).astype(BF16)
            outbuf[0:mine, cut] = part
            nearret[0:slots, cut] = part[0:slots]
        for c in back:
            c.start()

    def relayed_group(g):
        low = mine + 2 * g * slots

        @pl.when(outer)
        def _():
            for c in range(chunks):
                relay[g][c][0].wait_recv()

        for c in range(chunks):
            relay[g][c][2].wait_recv()
        into_hidden(low, 2 * slots)
        for c in range(chunks):
            cut = slice(c * tile, (c + 1) * tile)
            part = jnp.dot(hid[0:2 * slots, :], dbuf[:, cut], preferred_element_type=F32).astype(BF16)
            outbuf[low:low + 2 * slots, cut] = part
            farret[g, 0:slots, cut] = part[0:slots]

            @pl.when(inner)
            def _():
                answer[g][c][1].start()

            @pl.when(outer)
            def _():
                answer[g][c][2].start()
                answer[g][c][3].start()

    def send_home(g):
        @pl.when(inner)
        def _():
            unused, far0, far1 = one_hots(farid.at[g], partner, slots)
            w0, w1 = column(farrw[g, 0:1, :]), column(farrw[g, 1:2, :])
            for c in range(chunks):
                cut = slice(c * tile, (c + 1) * tile)
                for r in range(1, near):
                    answer[g][c][r].wait_recv()
                part = farret[g, :, cut]
                mixfar[g, :, cut] = (w0 * jnp.dot(far0, part, preferred_element_type=F32)
                                     + w1 * jnp.dot(far1, part, preferred_element_type=F32)).astype(BF16)
                home[g][c].start()

    relayed_group(0)
    near_group()
    send_home(0)
    relayed_group(1)
    send_home(1)

    w0, w1 = column(rwbuf[0:1, :]), column(rwbuf[1:2, :])
    for c in back:
        c.wait_recv()
    for c in range(chunks):
        cut = slice(c * tile, (c + 1) * tile)
        part = nearret[:, cut]
        nearsum[:, cut] = (w0 * jnp.dot(near0, part, preferred_element_type=F32)
                           + w1 * jnp.dot(near1, part, preferred_element_type=F32))
    for c in range(chunks):
        cut = slice(c * tile, (c + 1) * tile)
        home[0][c].wait_recv()
        out[:, cut] = (nearsum[:, cut] + mixback[:, cut].astype(F32)).astype(BF16)

    for c in meta + over + swap + direct + back:
        c.wait_send()

    @pl.when(inner)
    def _():
        for g in sides:
            for c in range(chunks):
                for copy in relay[g][c]:
                    copy.wait_send()
                answer[g][c][1].wait_send()
                home[g][c].wait_send()

    @pl.when(outer)
    def _():
        for g in sides:
            for c in range(chunks):
                answer[g][c][2].wait_send()
                answer[g][c][3].wait_send()


def fused(tokens, expert_ids, route_weights, gate_weight, up_weight, down_weight):
    toks, width = tokens.shape
    picks = expert_ids.shape[1]
    wide = lax.axis_size("wide")
    chips = wide // 2
    near = chips // 2
    slots = 4 * toks * picks // wide
    half = gate_weight.shape[1]
    rows = chips * slots
    mine = near * slots
    tile = 512
    chunks = width // tile
    vmem = pl.BlockSpec(memory_space=pltpu.VMEM)
    hbm = pl.BlockSpec(memory_space=pl.ANY)
    tok_like = pltpu.VMEM((toks, width), BF16)
    near_like = pltpu.VMEM((mine, width), BF16)
    all_like = pltpu.VMEM((rows, width), BF16)
    id_like = pltpu.VMEM((picks, toks), jnp.int32)
    rw_like = pltpu.VMEM((picks, toks), F32)
    sems = pltpu.SemaphoreType.DMA
    return pl.pallas_call(
        functools.partial(kernel, slots, tile),
        out_shape=jax.ShapeDtypeStruct((toks, width), BF16),
        in_specs=[hbm] * 6,
        out_specs=vmem,
        scratch_shapes=[tok_like, id_like, rw_like,
                        pltpu.VMEM((2, toks, width), BF16), pltpu.VMEM((2, picks, toks), jnp.int32),
                        pltpu.VMEM((2, picks, toks), F32), near_like, pltpu.VMEM((2, mine, width), BF16),
                        all_like, all_like, near_like, pltpu.VMEM((2, mine, width), BF16),
                        pltpu.VMEM((2, toks, width), BF16), tok_like, pltpu.VMEM((toks, width), F32)]
        + [pltpu.VMEM((2 * half, width), BF16)] * 3
        + [pltpu.VMEM((mine, 2 * half), BF16)]
        + [sems((6,)), sems((3,)), sems((3,)), sems((chunks,)), sems((2, chunks)), sems((2,)), sems((2, 2)),
           sems((near,)), sems((near,)), sems((2, near, chunks)), sems((2, 2, chunks)),
           sems((near,)), sems((near,)), sems((2, 2, chunks)), sems((2, near, chunks)),
           sems((2, chunks)), sems((chunks,))],
        compiler_params=pltpu.CompilerParams(
            collective_id=0, has_side_effects=True, vmem_limit_bytes=(53 * 1024 + 512) * 1024),
        cost_estimate=pl.CostEstimate(
            flops=12 * rows * half * width, bytes_accessed=6 * half * width + 4 * toks * width,
            transcendentals=2 * rows * half),
    )(tokens, expert_ids.T, route_weights.T, gate_weight, up_weight, down_weight)


def solution(mesh):
    in_specs = (
        P(("groups", "wide"), "narrow"),
        P(("groups", "wide"), None),
        P(("groups", "wide"), None),
        P("wide", "narrow", None),
        P("wide", "narrow", None),
        P("wide", "narrow", None),
    )
    out_specs = P(("groups", "wide"), "narrow")
    whole_rows = mesh.shape["narrow"] == 1 and mesh.shape["wide"] == 16
    return jax.shard_map(
        fused if whole_rows else per_device, mesh=mesh, in_specs=in_specs, out_specs=out_specs, check_vma=False
    )
```

```python
import functools

import jax
import jax.numpy as jnp
from jax import lax
from jax.experimental import pallas as pl
from jax.experimental.pallas import tpu as pltpu
from jax.sharding import PartitionSpec as P

F32 = jnp.float32
BF16 = jnp.bfloat16


def per_device(tokens, expert_ids, route_weights, gate_weight, up_weight, down_weight):
    tok_rows = tokens.shape[0]
    picks = expert_ids.shape[1]
    width_wide = lax.axis_size("wide")
    experts = width_wide // 2
    slots = 4 * tok_rows * picks // width_wide
    payload = lax.all_gather(tokens, "narrow", axis=1, tiled=True)
    feature_width = payload.shape[1]
    flat_ids = expert_ids.reshape(-1)
    flat_weights = route_weights.reshape(-1)
    onehot = (flat_ids[:, None] == jnp.arange(experts, dtype=jnp.int32)[None, :]).astype(jnp.int32)
    slot_rank = jnp.sum(jnp.cumsum(onehot, axis=0) * onehot, axis=1) - 1
    slot_place = flat_ids * slots + slot_rank
    token_source = jnp.arange(tok_rows * picks, dtype=jnp.int32) // picks
    slot_token = jnp.full((experts * slots,), tok_rows, jnp.int32).at[slot_place].set(token_source)
    padded = jnp.concatenate([payload, jnp.zeros((1, feature_width), payload.dtype)], axis=0)
    buffer = padded[slot_token].reshape(experts, slots, feature_width)
    outgoing = jnp.repeat(buffer, 2, axis=0)
    received = lax.all_to_all(outgoing, "wide", split_axis=0, concat_axis=0, tiled=True)
    model_width = received.shape[2]
    rows = received.reshape(width_wide * slots, model_width)
    gate = jnp.einsum("rd,hd->rh", rows, gate_weight[0], preferred_element_type=jnp.float32)
    up_part = jnp.einsum("rd,hd->rh", rows, up_weight[0], preferred_element_type=jnp.float32)
    hidden = (jax.nn.silu(gate) * up_part).astype(jnp.bfloat16)
    quarter_out = jnp.dot(hidden, down_weight[0], preferred_element_type=jnp.float32)
    quarter_blocks = quarter_out.reshape(width_wide, slots, model_width)
    returned = lax.all_to_all(quarter_blocks, "wide", split_axis=0, concat_axis=0, tiled=True)
    by_expert = jnp.sum(returned.reshape(experts, 2, slots, model_width), axis=1)
    pieces = by_expert[flat_ids, slot_rank]
    expert_total = lax.psum_scatter(pieces, "narrow", scatter_dimension=1, tiled=True)
    rounded = lax.optimization_barrier(expert_total.astype(jnp.bfloat16))
    pair_total = rounded.astype(jnp.float32) * flat_weights[:, None]
    column_width = pair_total.shape[1]
    mixed = jnp.sum(pair_total.reshape(tok_rows, picks, column_width), axis=1)
    return mixed.astype(jnp.bfloat16)


def flip(number, mask, bits):
    out = number
    for b in range(bits):
        if (mask >> b) & 1:
            bit = lax.rem(lax.div(number, 1 << b), 2)
            out = out + (1 - 2 * bit) * (1 << b)
    return out


def column(row):
    n = row.shape[1]
    same = lax.broadcasted_iota(jnp.int32, (n, n), 0) == lax.broadcasted_iota(jnp.int32, (n, n), 1)
    return jnp.sum(jnp.where(same, row, 0.0), axis=1, keepdims=True)


def one_hots(ids, experts, slots):
    toks = ids.shape[1]
    cols = len(experts) * slots
    id0 = column(ids[0:1, :].astype(F32))
    id1 = column(ids[1:2, :].astype(F32))
    col = lax.broadcasted_iota(jnp.int32, (toks, cols), 1)
    expert = jnp.zeros((toks, cols), F32)
    first = jnp.zeros((toks, cols), jnp.int32)
    for r, e in enumerate(experts):
        inside = (col >= r * slots) & (col < (r + 1) * slots)
        expert = jnp.where(inside, e.astype(F32), expert)
        first = jnp.where(inside, r * slots, first)
    pick0 = jnp.where(id0 == expert, 1.0, 0.0)
    pick1 = jnp.where(id1 == expert, 1.0, 0.0)
    named = pick0 + pick1
    before = jnp.where(lax.broadcasted_iota(jnp.int32, (toks, toks), 0)
                       > lax.broadcasted_iota(jnp.int32, (toks, toks), 1), 1.0, 0.0)
    rank = jnp.dot(before.astype(BF16), named.astype(BF16), preferred_element_type=F32)
    here = jnp.where(rank == (col - first).astype(F32), 1.0, 0.0)
    choose = jnp.transpose(here * named).astype(BF16)
    return choose, (here * pick0).astype(BF16), (here * pick1).astype(BF16)


def kernel(slots, tile, tok, ids, rw, gw, uw, dw, out,
           tokbuf, idbuf, rwbuf, fartok, farid, farrw, nearsend, relaysend, recvbuf, outbuf,
           nearret, farret, mixfar, mixback, nearsum, gbuf, ubuf, dbuf, hid,
           local_sem, w_send, w_recv, t_send, t_recv, m_send, m_recv, n_send, n_recv,
           l_send, l_recv, b_send, b_recv, f_send, f_recv, c_send, c_recv):
    near = 4
    half = gw.shape[1]
    width = tok.shape[1]
    chunks = width // tile
    mine = near * slots
    me = lax.axis_index("wide")
    chip = lax.div(me, 2)
    core = lax.rem(me, 2)
    z = lax.div(chip, 2)
    inner = lax.rem(z + 1, 4) >= 2
    outer = lax.rem(z + 1, 4) < 2
    slot = jnp.where(inner, 0, 1)
    sibling = 2 * chip + 1 - core
    partner = [flip(chip, r, 3) for r in range(near)]
    device = [2 * p + core for p in partner]
    across = [2 * flip(chip, 6, 3) + core, 2 * flip(chip, 4, 3) + core]
    relay_of_me = jnp.where(inner, across[0], across[1])

    def remote(src, dst, send, recv, to):
        return pltpu.make_async_remote_copy(src_ref=src, dst_ref=dst, send_sem=send, recv_sem=recv,
                                            device_id={"wide": to}, device_id_type=pl.DeviceIdType.MESH)

    barrier = pltpu.get_barrier_semaphore()
    for to in across + [sibling] + device[1:]:
        pl.semaphore_signal(barrier, inc=1, device_id={"wide": to}, device_id_type=pl.DeviceIdType.MESH)

    pairs = ((gw, gbuf), (uw, ubuf), (dw, dbuf))
    small = [pltpu.make_async_copy(src, dst, local_sem.at[3 + i])
             for i, (src, dst) in enumerate(((ids, idbuf), (rw, rwbuf), (tok, tokbuf)))]
    local = [pltpu.make_async_copy(src.at[0], dst.at[pl.ds(0, half)], local_sem.at[i])
             for i, (src, dst) in enumerate(pairs)]
    for c in small + local:
        c.start()

    span = [pl.ds(r * slots, slots) for r in range(2 * near)]
    cuts = [pl.ds(c * tile, tile) for c in range(chunks)]
    sides = range(2)

    def crossing(at):
        meta = [remote(ids, farid.at[at], m_send.at[0], m_recv.at[at, 0], relay_of_me),
                remote(rw, farrw.at[at], m_send.at[1], m_recv.at[at, 1], relay_of_me)]
        return meta, [remote(tok.at[:, cuts[c]], fartok.at[at, :, cuts[c]], t_send.at[c], t_recv.at[at, c],
                             relay_of_me) for c in range(chunks)]

    meta, over = crossing(slot)
    arriving = [crossing(g) for g in sides]
    swap = [remote(src.at[0], dst.at[pl.ds(half, half)], w_send.at[i], w_recv.at[i], sibling)
            for i, (src, dst) in enumerate(pairs)]
    direct = [remote(nearsend.at[span[r]], recvbuf.at[span[r]], n_send.at[r], n_recv.at[r], device[r])
              for r in range(1, near)]
    back = [remote(outbuf.at[span[r]], nearret.at[span[r]], b_send.at[r], b_recv.at[r], device[r])
            for r in range(1, near)]

    def block(g, i):
        return span[near + 2 * g + i]

    relay = [[[remote(relaysend.at[g, span[r], cuts[c]], recvbuf.at[block(g, r % 2), cuts[c]],
                      l_send.at[g, r, c], l_recv.at[g, r % 2, c], device[r]) for r in (2, 3, 1)]
              for c in range(chunks)] for g in sides]
    answer = [[[None] + [remote(outbuf.at[block(g, r % 2), cuts[c]], farret.at[g, span[r], cuts[c]],
                                f_send.at[g, r % 2, c], f_recv.at[g, r, c], device[r]) for r in range(1, near)]
               for c in range(chunks)] for g in sides]
    home = [[remote(mixfar.at[g, :, cuts[c]], mixback.at[:, cuts[c]], c_send.at[g, c], c_recv.at[c], across[g])
             for c in range(chunks)] for g in sides]

    pl.semaphore_wait(barrier, near + 2)

    @pl.when(inner)
    def _():
        for c in meta + over:
            c.start()

    for c in small:
        c.wait()
    choose, near0, near1 = one_hots(idbuf, partner, slots)
    for c in range(chunks):
        cut = slice(c * tile, (c + 1) * tile)
        picked = jnp.dot(choose, tokbuf[:, cut], preferred_element_type=F32).astype(BF16)
        nearsend[:, cut] = picked
        recvbuf[0:slots, cut] = picked[0:slots]
    for c in direct:
        c.start()

    @pl.when(outer)
    def _():
        for c in meta + over:
            c.start()

    for c in swap:
        c.start()

    @pl.when(inner)
    def _():
        for g in sides:
            for c in arriving[g][0]:
                c.wait_recv()
            choose, unused0, unused1 = one_hots(farid.at[g], partner, slots)
            for c in range(chunks):
                cut = slice(c * tile, (c + 1) * tile)
                arriving[g][1][c].wait_recv()
                picked = jnp.dot(choose, fartok[g, :, cut], preferred_element_type=F32).astype(BF16)
                relaysend[g, :, cut] = picked
                low = mine + 2 * g * slots
                recvbuf[low:low + slots, cut] = picked[0:slots]
                for copy in relay[g][c]:
                    copy.start()

    for c in local:
        c.wait()
    for c in swap:
        c.wait_recv()

    hid_tile = 256

    def into_hidden(base, rows):
        @pl.loop(0, 2 * half // hid_tile)
        def _(i):
            at = pl.ds(pl.multiple_of(i * hid_tile, hid_tile), hid_tile)
            x = recvbuf[base:base + rows, :]
            dims = (((1,), (1,)), ((), ()))
            gate = lax.dot_general(x, gbuf[at, :], dims, preferred_element_type=F32)
            up = lax.dot_general(x, ubuf[at, :], dims, preferred_element_type=F32)
            hid[0:rows, at] = (gate / (1.0 + jnp.exp(-gate)) * up).astype(BF16)

    def near_group():
        for c in direct:
            c.wait_recv()
        into_hidden(0, mine)
        for c in range(chunks):
            cut = slice(c * tile, (c + 1) * tile)
            part = jnp.dot(hid[...], dbuf[:, cut], preferred_element_type=F32).astype(BF16)
            outbuf[0:mine, cut] = part
            nearret[0:slots, cut] = part[0:slots]
        for c in back:
            c.start()

    def relayed_group(g):
        low = mine + 2 * g * slots

        @pl.when(outer)
        def _():
            for c in range(chunks):
                relay[g][c][0].wait_recv()

        for c in range(chunks):
            relay[g][c][2].wait_recv()
        into_hidden(low, 2 * slots)
        for c in range(chunks):
            cut = slice(c * tile, (c + 1) * tile)
            part = jnp.dot(hid[0:2 * slots, :], dbuf[:, cut], preferred_element_type=F32).astype(BF16)
            outbuf[low:low + 2 * slots, cut] = part
            farret[g, 0:slots, cut] = part[0:slots]

            @pl.when(inner)
            def _():
                answer[g][c][1].start()

            @pl.when(outer)
            def _():
                answer[g][c][2].start()
                answer[g][c][3].start()

    def send_home(g):
        @pl.when(inner)
        def _():
            unused, far0, far1 = one_hots(farid.at[g], partner, slots)
            w0, w1 = column(farrw[g, 0:1, :]), column(farrw[g, 1:2, :])
            for c in range(chunks):
                cut = slice(c * tile, (c + 1) * tile)
                for r in range(1, near):
                    answer[g][c][r].wait_recv()
                part = farret[g, :, cut]
                mixfar[g, :, cut] = (w0 * jnp.dot(far0, part, preferred_element_type=F32)
                                     + w1 * jnp.dot(far1, part, preferred_element_type=F32)).astype(BF16)
                home[g][c].start()

    near_group()
    relayed_group(0)
    send_home(0)
    relayed_group(1)
    send_home(1)

    w0, w1 = column(rwbuf[0:1, :]), column(rwbuf[1:2, :])
    for c in back:
        c.wait_recv()
    for c in range(chunks):
        cut = slice(c * tile, (c + 1) * tile)
        part = nearret[:, cut]
        nearsum[:, cut] = (w0 * jnp.dot(near0, part, preferred_element_type=F32)
                           + w1 * jnp.dot(near1, part, preferred_element_type=F32))
    for c in range(chunks):
        cut = slice(c * tile, (c + 1) * tile)
        home[0][c].wait_recv()
        out[:, cut] = (nearsum[:, cut] + mixback[:, cut].astype(F32)).astype(BF16)

    for c in meta + over + swap + direct + back:
        c.wait_send()

    @pl.when(inner)
    def _():
        for g in sides:
            for c in range(chunks):
                for copy in relay[g][c]:
                    copy.wait_send()
                answer[g][c][1].wait_send()
                home[g][c].wait_send()

    @pl.when(outer)
    def _():
        for g in sides:
            for c in range(chunks):
                answer[g][c][2].wait_send()
                answer[g][c][3].wait_send()


def fused(tokens, expert_ids, route_weights, gate_weight, up_weight, down_weight):
    toks, width = tokens.shape
    picks = expert_ids.shape[1]
    wide = lax.axis_size("wide")
    chips = wide // 2
    near = chips // 2
    slots = 4 * toks * picks // wide
    half = gate_weight.shape[1]
    rows = chips * slots
    mine = near * slots
    tile = 512
    chunks = width // tile
    vmem = pl.BlockSpec(memory_space=pltpu.VMEM)
    hbm = pl.BlockSpec(memory_space=pl.ANY)
    tok_like = pltpu.VMEM((toks, width), BF16)
    near_like = pltpu.VMEM((mine, width), BF16)
    all_like = pltpu.VMEM((rows, width), BF16)
    id_like = pltpu.VMEM((picks, toks), jnp.int32)
    rw_like = pltpu.VMEM((picks, toks), F32)
    sems = pltpu.SemaphoreType.DMA
    return pl.pallas_call(
        functools.partial(kernel, slots, tile),
        out_shape=jax.ShapeDtypeStruct((toks, width), BF16),
        in_specs=[hbm] * 6,
        out_specs=vmem,
        scratch_shapes=[tok_like, id_like, rw_like,
                        pltpu.VMEM((2, toks, width), BF16), pltpu.VMEM((2, picks, toks), jnp.int32),
                        pltpu.VMEM((2, picks, toks), F32), near_like, pltpu.VMEM((2, mine, width), BF16),
                        all_like, all_like, near_like, pltpu.VMEM((2, mine, width), BF16),
                        pltpu.VMEM((2, toks, width), BF16), tok_like, pltpu.VMEM((toks, width), F32)]
        + [pltpu.VMEM((2 * half, width), BF16)] * 3
        + [pltpu.VMEM((mine, 2 * half), BF16)]
        + [sems((6,)), sems((3,)), sems((3,)), sems((chunks,)), sems((2, chunks)), sems((2,)), sems((2, 2)),
           sems((near,)), sems((near,)), sems((2, near, chunks)), sems((2, 2, chunks)),
           sems((near,)), sems((near,)), sems((2, 2, chunks)), sems((2, near, chunks)),
           sems((2, chunks)), sems((chunks,))],
        compiler_params=pltpu.CompilerParams(
            collective_id=0, has_side_effects=True, vmem_limit_bytes=(53 * 1024 + 512) * 1024),
        cost_estimate=pl.CostEstimate(
            flops=12 * rows * half * width, bytes_accessed=6 * half * width + 4 * toks * width,
            transcendentals=2 * rows * half),
    )(tokens, expert_ids.T, route_weights.T, gate_weight, up_weight, down_weight)


def solution(mesh):
    in_specs = (
        P(("groups", "wide"), "narrow"),
        P(("groups", "wide"), None),
        P(("groups", "wide"), None),
        P("wide", "narrow", None),
        P("wide", "narrow", None),
        P("wide", "narrow", None),
    )
    out_specs = P(("groups", "wide"), "narrow")
    whole_rows = mesh.shape["narrow"] == 1 and mesh.shape["wide"] == 16
    return jax.shard_map(
        fused if whole_rows else per_device, mesh=mesh, in_specs=in_specs, out_specs=out_specs, check_vma=False
    )
```

```python
import functools

import jax
import jax.numpy as jnp
from jax import lax
from jax.experimental import pallas as pl
from jax.experimental.pallas import tpu as pltpu
from jax.sharding import PartitionSpec as P

F32 = jnp.float32
BF16 = jnp.bfloat16


def per_device(tokens, expert_ids, route_weights, gate_weight, up_weight, down_weight):
    tok_rows = tokens.shape[0]
    picks = expert_ids.shape[1]
    width_wide = lax.axis_size("wide")
    experts = width_wide // 2
    slots = 4 * tok_rows * picks // width_wide
    payload = lax.all_gather(tokens, "narrow", axis=1, tiled=True)
    feature_width = payload.shape[1]
    flat_ids = expert_ids.reshape(-1)
    flat_weights = route_weights.reshape(-1)
    onehot = (flat_ids[:, None] == jnp.arange(experts, dtype=jnp.int32)[None, :]).astype(jnp.int32)
    slot_rank = jnp.sum(jnp.cumsum(onehot, axis=0) * onehot, axis=1) - 1
    slot_place = flat_ids * slots + slot_rank
    token_source = jnp.arange(tok_rows * picks, dtype=jnp.int32) // picks
    slot_token = jnp.full((experts * slots,), tok_rows, jnp.int32).at[slot_place].set(token_source)
    padded = jnp.concatenate([payload, jnp.zeros((1, feature_width), payload.dtype)], axis=0)
    buffer = padded[slot_token].reshape(experts, slots, feature_width)
    outgoing = jnp.repeat(buffer, 2, axis=0)
    received = lax.all_to_all(outgoing, "wide", split_axis=0, concat_axis=0, tiled=True)
    model_width = received.shape[2]
    rows = received.reshape(width_wide * slots, model_width)
    gate = jnp.einsum("rd,hd->rh", rows, gate_weight[0], preferred_element_type=jnp.float32)
    up_part = jnp.einsum("rd,hd->rh", rows, up_weight[0], preferred_element_type=jnp.float32)
    hidden = (jax.nn.silu(gate) * up_part).astype(jnp.bfloat16)
    quarter_out = jnp.dot(hidden, down_weight[0], preferred_element_type=jnp.float32)
    quarter_blocks = quarter_out.reshape(width_wide, slots, model_width)
    returned = lax.all_to_all(quarter_blocks, "wide", split_axis=0, concat_axis=0, tiled=True)
    by_expert = jnp.sum(returned.reshape(experts, 2, slots, model_width), axis=1)
    pieces = by_expert[flat_ids, slot_rank]
    expert_total = lax.psum_scatter(pieces, "narrow", scatter_dimension=1, tiled=True)
    rounded = lax.optimization_barrier(expert_total.astype(jnp.bfloat16))
    pair_total = rounded.astype(jnp.float32) * flat_weights[:, None]
    column_width = pair_total.shape[1]
    mixed = jnp.sum(pair_total.reshape(tok_rows, picks, column_width), axis=1)
    return mixed.astype(jnp.bfloat16)


def flip(number, mask, bits):
    out = number
    for b in range(bits):
        if (mask >> b) & 1:
            bit = lax.rem(lax.div(number, 1 << b), 2)
            out = out + (1 - 2 * bit) * (1 << b)
    return out


def column(row):
    n = row.shape[1]
    same = lax.broadcasted_iota(jnp.int32, (n, n), 0) == lax.broadcasted_iota(jnp.int32, (n, n), 1)
    return jnp.sum(jnp.where(same, row, 0.0), axis=1, keepdims=True)


def one_hots(ids, experts, slots):
    toks = ids.shape[1]
    cols = len(experts) * slots
    id0 = column(ids[0:1, :].astype(F32))
    id1 = column(ids[1:2, :].astype(F32))
    col = lax.broadcasted_iota(jnp.int32, (toks, cols), 1)
    expert = jnp.zeros((toks, cols), F32)
    first = jnp.zeros((toks, cols), jnp.int32)
    for r, e in enumerate(experts):
        inside = (col >= r * slots) & (col < (r + 1) * slots)
        expert = jnp.where(inside, e.astype(F32), expert)
        first = jnp.where(inside, r * slots, first)
    pick0 = jnp.where(id0 == expert, 1.0, 0.0)
    pick1 = jnp.where(id1 == expert, 1.0, 0.0)
    named = pick0 + pick1
    before = jnp.where(lax.broadcasted_iota(jnp.int32, (toks, toks), 0)
                       > lax.broadcasted_iota(jnp.int32, (toks, toks), 1), 1.0, 0.0)
    rank = jnp.dot(before.astype(BF16), named.astype(BF16), preferred_element_type=F32)
    here = jnp.where(rank == (col - first).astype(F32), 1.0, 0.0)
    choose = jnp.transpose(here * named).astype(BF16)
    return choose, (here * pick0).astype(BF16), (here * pick1).astype(BF16)


def kernel(slots, tile, tok, ids, rw, gw, uw, dw, out,
           tokbuf, idbuf, rwbuf, fartok, farid, farrw, nearsend, relaysend, recvbuf, outbuf,
           nearret, farret, mixfar, mixback, nearsum, gbuf, ubuf, dbuf, hid,
           local_sem, w_send, w_recv, t_send, t_recv, m_send, m_recv, n_send, n_recv,
           l_send, l_recv, b_send, b_recv, f_send, f_recv, c_send, c_recv):
    near = 4
    half = gw.shape[1]
    width = tok.shape[1]
    chunks = width // tile
    mine = near * slots
    me = lax.axis_index("wide")
    chip = lax.div(me, 2)
    core = lax.rem(me, 2)
    z = lax.div(chip, 2)
    inner = lax.rem(z + 1, 4) >= 2
    outer = lax.rem(z + 1, 4) < 2
    slot = jnp.where(inner, 0, 1)
    sibling = 2 * chip + 1 - core
    partner = [flip(chip, r, 3) for r in range(near)]
    device = [2 * p + core for p in partner]
    across = [2 * flip(chip, 6, 3) + core, 2 * flip(chip, 4, 3) + core]
    relay_of_me = jnp.where(inner, across[0], across[1])

    def remote(src, dst, send, recv, to):
        return pltpu.make_async_remote_copy(src_ref=src, dst_ref=dst, send_sem=send, recv_sem=recv,
                                            device_id={"wide": to}, device_id_type=pl.DeviceIdType.MESH)

    barrier = pltpu.get_barrier_semaphore()
    for to in across + [sibling] + device[1:]:
        pl.semaphore_signal(barrier, inc=1, device_id={"wide": to}, device_id_type=pl.DeviceIdType.MESH)

    pairs = ((gw, gbuf), (uw, ubuf), (dw, dbuf))
    small = [pltpu.make_async_copy(src, dst, local_sem.at[3 + i])
             for i, (src, dst) in enumerate(((ids, idbuf), (rw, rwbuf), (tok, tokbuf)))]
    local = [pltpu.make_async_copy(src.at[0], dst.at[pl.ds(0, half)], local_sem.at[i])
             for i, (src, dst) in enumerate(pairs)]
    for c in small + local:
        c.start()

    span = [pl.ds(r * slots, slots) for r in range(2 * near)]
    cuts = [pl.ds(c * tile, tile) for c in range(chunks)]
    sides = range(2)

    def crossing(at):
        meta = [remote(ids, farid.at[at], m_send.at[0], m_recv.at[at, 0], relay_of_me),
                remote(rw, farrw.at[at], m_send.at[1], m_recv.at[at, 1], relay_of_me)]
        return meta, [remote(tok.at[:, cuts[c]], fartok.at[at, :, cuts[c]], t_send.at[c], t_recv.at[at, c],
                             relay_of_me) for c in range(chunks)]

    meta, over = crossing(slot)
    arriving = [crossing(g) for g in sides]
    swap = [remote(src.at[0], dst.at[pl.ds(half, half)], w_send.at[i], w_recv.at[i], sibling)
            for i, (src, dst) in enumerate(pairs)]
    direct = [remote(nearsend.at[span[r]], recvbuf.at[span[r]], n_send.at[r], n_recv.at[r], device[r])
              for r in range(1, near)]
    back = [remote(outbuf.at[span[r]], nearret.at[span[r]], b_send.at[r], b_recv.at[r], device[r])
            for r in range(1, near)]

    def block(g, i):
        return span[near + 2 * g + i]

    relay = [[[remote(relaysend.at[g, span[r], cuts[c]], recvbuf.at[block(g, r % 2), cuts[c]],
                      l_send.at[g, r, c], l_recv.at[g, r % 2, c], device[r]) for r in (2, 3, 1)]
              for c in range(chunks)] for g in sides]
    answer = [[[None] + [remote(outbuf.at[block(g, r % 2), cuts[c]], farret.at[g, span[r], cuts[c]],
                                f_send.at[g, r % 2, c], f_recv.at[g, r, c], device[r]) for r in range(1, near)]
               for c in range(chunks)] for g in sides]
    home = [[remote(mixfar.at[g, :, cuts[c]], mixback.at[:, cuts[c]], c_send.at[g, c], c_recv.at[c], across[g])
             for c in range(chunks)] for g in sides]

    pl.semaphore_wait(barrier, near + 2)

    @pl.when(inner)
    def _():
        for c in meta + over:
            c.start()

    for c in small:
        c.wait()
    choose, near0, near1 = one_hots(idbuf, partner, slots)
    for c in range(chunks):
        cut = slice(c * tile, (c + 1) * tile)
        picked = jnp.dot(choose, tokbuf[:, cut], preferred_element_type=F32).astype(BF16)
        nearsend[:, cut] = picked
        recvbuf[0:slots, cut] = picked[0:slots]
    for c in direct:
        c.start()

    @pl.when(outer)
    def _():
        for c in meta + over:
            c.start()

    for c in swap:
        c.start()

    @pl.when(inner)
    def _():
        for g in sides:
            for c in arriving[g][0]:
                c.wait_recv()
            choose, unused0, unused1 = one_hots(farid.at[g], partner, slots)
            for c in range(chunks):
                cut = slice(c * tile, (c + 1) * tile)
                arriving[g][1][c].wait_recv()
                picked = jnp.dot(choose, fartok[g, :, cut], preferred_element_type=F32).astype(BF16)
                relaysend[g, :, cut] = picked
                low = mine + 2 * g * slots
                recvbuf[low:low + slots, cut] = picked[0:slots]
                for copy in relay[g][c]:
                    copy.start()

    for c in local:
        c.wait()
    for c in swap:
        c.wait_recv()

    hid_tile = 256

    def into_hidden(base, rows):
        @pl.loop(0, 2 * half // hid_tile)
        def _(i):
            at = pl.ds(pl.multiple_of(i * hid_tile, hid_tile), hid_tile)
            x = recvbuf[base:base + rows, :]
            dims = (((1,), (1,)), ((), ()))
            gate = lax.dot_general(x, gbuf[at, :], dims, preferred_element_type=F32)
            up = lax.dot_general(x, ubuf[at, :], dims, preferred_element_type=F32)
            hid[0:rows, at] = (gate / (1.0 + jnp.exp(-gate)) * up).astype(BF16)

    def group(low, rows, g):
        @pl.when(outer)
        def _():
            for c in range(chunks):
                relay[g][c][0].wait_recv()

        for c in range(chunks):
            relay[g][c][2].wait_recv()
        into_hidden(low, rows)
        at = rows - 2 * slots
        for c in range(chunks):
            cut = slice(c * tile, (c + 1) * tile)
            part = jnp.dot(hid[0:rows, :], dbuf[:, cut], preferred_element_type=F32).astype(BF16)
            outbuf[low:low + rows, cut] = part
            farret[g, 0:slots, cut] = part[at:at + slots]
            if g == 0:
                nearret[0:slots, cut] = part[0:slots]

            @pl.when(inner)
            def _():
                answer[g][c][1].start()

            @pl.when(outer)
            def _():
                answer[g][c][2].start()
                answer[g][c][3].start()

    def send_home(g):
        @pl.when(inner)
        def _():
            unused, far0, far1 = one_hots(farid.at[g], partner, slots)
            w0, w1 = column(farrw[g, 0:1, :]), column(farrw[g, 1:2, :])
            for c in range(chunks):
                cut = slice(c * tile, (c + 1) * tile)
                for r in range(1, near):
                    answer[g][c][r].wait_recv()
                part = farret[g, :, cut]
                mixfar[g, :, cut] = (w0 * jnp.dot(far0, part, preferred_element_type=F32)
                                     + w1 * jnp.dot(far1, part, preferred_element_type=F32)).astype(BF16)
                home[g][c].start()

    for c in direct:
        c.wait_recv()
    group(0, mine + 2 * slots, 0)
    for c in back:
        c.start()
    send_home(0)
    group(mine + 2 * slots, 2 * slots, 1)
    send_home(1)

    w0, w1 = column(rwbuf[0:1, :]), column(rwbuf[1:2, :])
    for c in back:
        c.wait_recv()
    for c in range(chunks):
        cut = slice(c * tile, (c + 1) * tile)
        part = nearret[:, cut]
        nearsum[:, cut] = (w0 * jnp.dot(near0, part, preferred_element_type=F32)
                           + w1 * jnp.dot(near1, part, preferred_element_type=F32))
    for c in range(chunks):
        cut = slice(c * tile, (c + 1) * tile)
        home[0][c].wait_recv()
        out[:, cut] = (nearsum[:, cut] + mixback[:, cut].astype(F32)).astype(BF16)

    for c in meta + over + swap + direct + back:
        c.wait_send()

    @pl.when(inner)
    def _():
        for g in sides:
            for c in range(chunks):
                for copy in relay[g][c]:
                    copy.wait_send()
                answer[g][c][1].wait_send()
                home[g][c].wait_send()

    @pl.when(outer)
    def _():
        for g in sides:
            for c in range(chunks):
                answer[g][c][2].wait_send()
                answer[g][c][3].wait_send()


def fused(tokens, expert_ids, route_weights, gate_weight, up_weight, down_weight):
    toks, width = tokens.shape
    picks = expert_ids.shape[1]
    wide = lax.axis_size("wide")
    chips = wide // 2
    near = chips // 2
    slots = 4 * toks * picks // wide
    half = gate_weight.shape[1]
    rows = chips * slots
    mine = near * slots
    tile = 512
    chunks = width // tile
    vmem = pl.BlockSpec(memory_space=pltpu.VMEM)
    hbm = pl.BlockSpec(memory_space=pl.ANY)
    tok_like = pltpu.VMEM((toks, width), BF16)
    near_like = pltpu.VMEM((mine, width), BF16)
    all_like = pltpu.VMEM((rows, width), BF16)
    id_like = pltpu.VMEM((picks, toks), jnp.int32)
    rw_like = pltpu.VMEM((picks, toks), F32)
    sems = pltpu.SemaphoreType.DMA
    return pl.pallas_call(
        functools.partial(kernel, slots, tile),
        out_shape=jax.ShapeDtypeStruct((toks, width), BF16),
        in_specs=[hbm] * 6,
        out_specs=vmem,
        scratch_shapes=[tok_like, id_like, rw_like,
                        pltpu.VMEM((2, toks, width), BF16), pltpu.VMEM((2, picks, toks), jnp.int32),
                        pltpu.VMEM((2, picks, toks), F32), near_like, pltpu.VMEM((2, mine, width), BF16),
                        all_like, all_like, near_like, pltpu.VMEM((2, mine, width), BF16),
                        pltpu.VMEM((2, toks, width), BF16), tok_like, pltpu.VMEM((toks, width), F32)]
        + [pltpu.VMEM((2 * half, width), BF16)] * 3
        + [pltpu.VMEM((mine + 2 * slots, 2 * half), BF16)]
        + [sems((6,)), sems((3,)), sems((3,)), sems((chunks,)), sems((2, chunks)), sems((2,)), sems((2, 2)),
           sems((near,)), sems((near,)), sems((2, near, chunks)), sems((2, 2, chunks)),
           sems((near,)), sems((near,)), sems((2, 2, chunks)), sems((2, near, chunks)),
           sems((2, chunks)), sems((chunks,))],
        compiler_params=pltpu.CompilerParams(
            collective_id=0, has_side_effects=True, vmem_limit_bytes=(53 * 1024 + 512) * 1024),
        cost_estimate=pl.CostEstimate(
            flops=12 * rows * half * width, bytes_accessed=6 * half * width + 4 * toks * width,
            transcendentals=2 * rows * half),
    )(tokens, expert_ids.T, route_weights.T, gate_weight, up_weight, down_weight)


def solution(mesh):
    in_specs = (
        P(("groups", "wide"), "narrow"),
        P(("groups", "wide"), None),
        P(("groups", "wide"), None),
        P("wide", "narrow", None),
        P("wide", "narrow", None),
        P("wide", "narrow", None),
    )
    out_specs = P(("groups", "wide"), "narrow")
    whole_rows = mesh.shape["narrow"] == 1 and mesh.shape["wide"] == 16
    return jax.shard_map(
        fused if whole_rows else per_device, mesh=mesh, in_specs=in_specs, out_specs=out_specs, check_vma=False
    )
```

```python
import functools

import jax
import jax.numpy as jnp
from jax import lax
from jax.experimental import pallas as pl
from jax.experimental.pallas import tpu as pltpu
from jax.sharding import PartitionSpec as P

F32 = jnp.float32
BF16 = jnp.bfloat16


def per_device(tokens, expert_ids, route_weights, gate_weight, up_weight, down_weight):
    tok_rows = tokens.shape[0]
    picks = expert_ids.shape[1]
    width_wide = lax.axis_size("wide")
    experts = width_wide // 2
    slots = 4 * tok_rows * picks // width_wide
    payload = lax.all_gather(tokens, "narrow", axis=1, tiled=True)
    feature_width = payload.shape[1]
    flat_ids = expert_ids.reshape(-1)
    flat_weights = route_weights.reshape(-1)
    onehot = (flat_ids[:, None] == jnp.arange(experts, dtype=jnp.int32)[None, :]).astype(jnp.int32)
    slot_rank = jnp.sum(jnp.cumsum(onehot, axis=0) * onehot, axis=1) - 1
    slot_place = flat_ids * slots + slot_rank
    token_source = jnp.arange(tok_rows * picks, dtype=jnp.int32) // picks
    slot_token = jnp.full((experts * slots,), tok_rows, jnp.int32).at[slot_place].set(token_source)
    padded = jnp.concatenate([payload, jnp.zeros((1, feature_width), payload.dtype)], axis=0)
    buffer = padded[slot_token].reshape(experts, slots, feature_width)
    outgoing = jnp.repeat(buffer, 2, axis=0)
    received = lax.all_to_all(outgoing, "wide", split_axis=0, concat_axis=0, tiled=True)
    model_width = received.shape[2]
    rows = received.reshape(width_wide * slots, model_width)
    gate = jnp.einsum("rd,hd->rh", rows, gate_weight[0], preferred_element_type=jnp.float32)
    up_part = jnp.einsum("rd,hd->rh", rows, up_weight[0], preferred_element_type=jnp.float32)
    hidden = (jax.nn.silu(gate) * up_part).astype(jnp.bfloat16)
    quarter_out = jnp.dot(hidden, down_weight[0], preferred_element_type=jnp.float32)
    quarter_blocks = quarter_out.reshape(width_wide, slots, model_width)
    returned = lax.all_to_all(quarter_blocks, "wide", split_axis=0, concat_axis=0, tiled=True)
    by_expert = jnp.sum(returned.reshape(experts, 2, slots, model_width), axis=1)
    pieces = by_expert[flat_ids, slot_rank]
    expert_total = lax.psum_scatter(pieces, "narrow", scatter_dimension=1, tiled=True)
    rounded = lax.optimization_barrier(expert_total.astype(jnp.bfloat16))
    pair_total = rounded.astype(jnp.float32) * flat_weights[:, None]
    column_width = pair_total.shape[1]
    mixed = jnp.sum(pair_total.reshape(tok_rows, picks, column_width), axis=1)
    return mixed.astype(jnp.bfloat16)


def flip(number, mask, bits):
    out = number
    for b in range(bits):
        if (mask >> b) & 1:
            bit = lax.rem(lax.div(number, 1 << b), 2)
            out = out + (1 - 2 * bit) * (1 << b)
    return out


def column(row):
    n = row.shape[1]
    same = lax.broadcasted_iota(jnp.int32, (n, n), 0) == lax.broadcasted_iota(jnp.int32, (n, n), 1)
    return jnp.sum(jnp.where(same, row, 0.0), axis=1, keepdims=True)


def one_hots(ids, experts, slots):
    toks = ids.shape[1]
    cols = len(experts) * slots
    id0 = column(ids[0:1, :].astype(F32))
    id1 = column(ids[1:2, :].astype(F32))
    col = lax.broadcasted_iota(jnp.int32, (toks, cols), 1)
    expert = jnp.zeros((toks, cols), F32)
    first = jnp.zeros((toks, cols), jnp.int32)
    for r, e in enumerate(experts):
        inside = (col >= r * slots) & (col < (r + 1) * slots)
        expert = jnp.where(inside, e.astype(F32), expert)
        first = jnp.where(inside, r * slots, first)
    pick0 = jnp.where(id0 == expert, 1.0, 0.0)
    pick1 = jnp.where(id1 == expert, 1.0, 0.0)
    named = pick0 + pick1
    before = jnp.where(lax.broadcasted_iota(jnp.int32, (toks, toks), 0)
                       > lax.broadcasted_iota(jnp.int32, (toks, toks), 1), 1.0, 0.0)
    rank = jnp.dot(before.astype(BF16), named.astype(BF16), preferred_element_type=F32)
    here = jnp.where(rank == (col - first).astype(F32), 1.0, 0.0)
    choose = jnp.transpose(here * named).astype(BF16)
    return choose, (here * pick0).astype(BF16), (here * pick1).astype(BF16)


def kernel(slots, tile, tok, ids, rw, gw, uw, dw, out,
           tokbuf, idbuf, rwbuf, fartok, farid, farrw, nearsend, relaysend, recvbuf, outbuf,
           nearret, farret, mixfar, mixback, nearsum, gbuf, ubuf, dbuf, hid,
           local_sem, w_send, w_recv, t_send, t_recv, m_send, m_recv, n_send, n_recv,
           l_send, l_recv, b_send, b_recv, f_send, f_recv, c_send, c_recv):
    near = 4
    half = gw.shape[1]
    width = tok.shape[1]
    chunks = width // tile
    mine = near * slots
    me = lax.axis_index("wide")
    chip = lax.div(me, 2)
    core = lax.rem(me, 2)
    z = lax.div(chip, 2)
    inner = lax.rem(z + 1, 4) >= 2
    outer = lax.rem(z + 1, 4) < 2
    slot = jnp.where(inner, 0, 1)
    sibling = 2 * chip + 1 - core
    partner = [flip(chip, r, 3) for r in range(near)]
    device = [2 * p + core for p in partner]
    across = [2 * flip(chip, 6, 3) + core, 2 * flip(chip, 4, 3) + core]
    relay_of_me = jnp.where(inner, across[0], across[1])

    def remote(src, dst, send, recv, to):
        return pltpu.make_async_remote_copy(src_ref=src, dst_ref=dst, send_sem=send, recv_sem=recv,
                                            device_id={"wide": to}, device_id_type=pl.DeviceIdType.MESH)

    barrier = pltpu.get_barrier_semaphore()
    for to in across + [sibling] + device[1:]:
        pl.semaphore_signal(barrier, inc=1, device_id={"wide": to}, device_id_type=pl.DeviceIdType.MESH)

    pairs = ((gw, gbuf), (uw, ubuf), (dw, dbuf))
    small = [pltpu.make_async_copy(src, dst, local_sem.at[3 + i])
             for i, (src, dst) in enumerate(((ids, idbuf), (rw, rwbuf), (tok, tokbuf)))]
    local = [pltpu.make_async_copy(src.at[0], dst.at[pl.ds(0, half)], local_sem.at[i])
             for i, (src, dst) in enumerate(pairs)]
    for c in small + local:
        c.start()

    span = [pl.ds(r * slots, slots) for r in range(2 * near)]
    cuts = [pl.ds(c * tile, tile) for c in range(chunks)]
    sides = range(2)

    def crossing(at):
        meta = [remote(ids, farid.at[at], m_send.at[0], m_recv.at[at, 0], relay_of_me),
                remote(rw, farrw.at[at], m_send.at[1], m_recv.at[at, 1], relay_of_me)]
        return meta, [remote(tok.at[:, cuts[c]], fartok.at[at, :, cuts[c]], t_send.at[c], t_recv.at[at, c],
                             relay_of_me) for c in range(chunks)]

    meta, over = crossing(slot)
    arriving = [crossing(g) for g in sides]
    swap = [remote(src.at[0], dst.at[pl.ds(half, half)], w_send.at[i], w_recv.at[i], sibling)
            for i, (src, dst) in enumerate(pairs)]
    direct = [remote(nearsend.at[span[r]], recvbuf.at[span[r]], n_send.at[r], n_recv.at[r], device[r])
              for r in range(1, near)]
    back = [remote(outbuf.at[span[r]], nearret.at[span[r]], b_send.at[r], b_recv.at[r], device[r])
            for r in range(1, near)]

    def block(g, i):
        return span[near + 2 * g + i]

    relay = [[[remote(relaysend.at[g, span[r], cuts[c]], recvbuf.at[block(g, r % 2), cuts[c]],
                      l_send.at[g, r, c], l_recv.at[g, r % 2, c], device[r]) for r in (2, 3, 1)]
              for c in range(chunks)] for g in sides]
    answer = [[[None] + [remote(outbuf.at[block(g, r % 2), cuts[c]], farret.at[g, span[r], cuts[c]],
                                f_send.at[g, r % 2, c], f_recv.at[g, r, c], device[r]) for r in range(1, near)]
               for c in range(chunks)] for g in sides]
    home = [[remote(mixfar.at[g, :, cuts[c]], mixback.at[:, cuts[c]], c_send.at[g, c], c_recv.at[c], across[g])
             for c in range(chunks)] for g in sides]

    pl.semaphore_wait(barrier, near + 2)

    for c in meta + over:
        c.start()

    for c in small:
        c.wait()
    choose, near0, near1 = one_hots(idbuf, partner, slots)
    for c in range(chunks):
        cut = slice(c * tile, (c + 1) * tile)
        picked = jnp.dot(choose, tokbuf[:, cut], preferred_element_type=F32).astype(BF16)
        nearsend[:, cut] = picked
        recvbuf[0:slots, cut] = picked[0:slots]
    for c in direct:
        c.start()

    for c in swap:
        c.start()

    @pl.when(inner)
    def _():
        for g in sides:
            for c in arriving[g][0]:
                c.wait_recv()
            choose, unused0, unused1 = one_hots(farid.at[g], partner, slots)
            for c in range(chunks):
                cut = slice(c * tile, (c + 1) * tile)
                arriving[g][1][c].wait_recv()
                picked = jnp.dot(choose, fartok[g, :, cut], preferred_element_type=F32).astype(BF16)
                relaysend[g, :, cut] = picked
                low = mine + 2 * g * slots
                recvbuf[low:low + slots, cut] = picked[0:slots]
                for copy in relay[g][c]:
                    copy.start()

    for c in local:
        c.wait()
    for c in swap:
        c.wait_recv()

    hid_tile = 256

    def into_hidden(base, rows):
        @pl.loop(0, 2 * half // hid_tile)
        def _(i):
            at = pl.ds(pl.multiple_of(i * hid_tile, hid_tile), hid_tile)
            x = recvbuf[base:base + rows, :]
            dims = (((1,), (1,)), ((), ()))
            gate = lax.dot_general(x, gbuf[at, :], dims, preferred_element_type=F32)
            up = lax.dot_general(x, ubuf[at, :], dims, preferred_element_type=F32)
            hid[0:rows, at] = (gate / (1.0 + jnp.exp(-gate)) * up).astype(BF16)

    def near_group():
        for c in direct:
            c.wait_recv()
        into_hidden(0, mine)
        for c in range(chunks):
            cut = slice(c * tile, (c + 1) * tile)
            part = jnp.dot(hid[...], dbuf[:, cut], preferred_element_type=F32).astype(BF16)
            outbuf[0:mine, cut] = part
            nearret[0:slots, cut] = part[0:slots]
        for c in back:
            c.start()

    def relayed_group(g):
        low = mine + 2 * g * slots

        @pl.when(outer)
        def _():
            for c in range(chunks):
                relay[g][c][0].wait_recv()

        for c in range(chunks):
            relay[g][c][2].wait_recv()
        into_hidden(low, 2 * slots)
        for c in range(chunks):
            cut = slice(c * tile, (c + 1) * tile)
            part = jnp.dot(hid[0:2 * slots, :], dbuf[:, cut], preferred_element_type=F32).astype(BF16)
            outbuf[low:low + 2 * slots, cut] = part
            farret[g, 0:slots, cut] = part[0:slots]

            @pl.when(inner)
            def _():
                answer[g][c][1].start()

            @pl.when(outer)
            def _():
                answer[g][c][2].start()
                answer[g][c][3].start()

    def send_home(g):
        @pl.when(inner)
        def _():
            unused, far0, far1 = one_hots(farid.at[g], partner, slots)
            w0, w1 = column(farrw[g, 0:1, :]), column(farrw[g, 1:2, :])
            for c in range(chunks):
                cut = slice(c * tile, (c + 1) * tile)
                for r in range(1, near):
                    answer[g][c][r].wait_recv()
                part = farret[g, :, cut]
                mixfar[g, :, cut] = (w0 * jnp.dot(far0, part, preferred_element_type=F32)
                                     + w1 * jnp.dot(far1, part, preferred_element_type=F32)).astype(BF16)
                home[g][c].start()

    relayed_group(0)
    near_group()
    send_home(0)
    relayed_group(1)
    send_home(1)

    w0, w1 = column(rwbuf[0:1, :]), column(rwbuf[1:2, :])
    for c in back:
        c.wait_recv()
    for c in range(chunks):
        cut = slice(c * tile, (c + 1) * tile)
        part = nearret[:, cut]
        nearsum[:, cut] = (w0 * jnp.dot(near0, part, preferred_element_type=F32)
                           + w1 * jnp.dot(near1, part, preferred_element_type=F32))
    for c in range(chunks):
        cut = slice(c * tile, (c + 1) * tile)
        home[0][c].wait_recv()
        out[:, cut] = (nearsum[:, cut] + mixback[:, cut].astype(F32)).astype(BF16)

    for c in meta + over + swap + direct + back:
        c.wait_send()

    @pl.when(inner)
    def _():
        for g in sides:
            for c in range(chunks):
                for copy in relay[g][c]:
                    copy.wait_send()
                answer[g][c][1].wait_send()
                home[g][c].wait_send()

    @pl.when(outer)
    def _():
        for g in sides:
            for c in range(chunks):
                answer[g][c][2].wait_send()
                answer[g][c][3].wait_send()


def fused(tokens, expert_ids, route_weights, gate_weight, up_weight, down_weight):
    toks, width = tokens.shape
    picks = expert_ids.shape[1]
    wide = lax.axis_size("wide")
    chips = wide // 2
    near = chips // 2
    slots = 4 * toks * picks // wide
    half = gate_weight.shape[1]
    rows = chips * slots
    mine = near * slots
    tile = 512
    chunks = width // tile
    vmem = pl.BlockSpec(memory_space=pltpu.VMEM)
    hbm = pl.BlockSpec(memory_space=pl.ANY)
    tok_like = pltpu.VMEM((toks, width), BF16)
    near_like = pltpu.VMEM((mine, width), BF16)
    all_like = pltpu.VMEM((rows, width), BF16)
    id_like = pltpu.VMEM((picks, toks), jnp.int32)
    rw_like = pltpu.VMEM((picks, toks), F32)
    sems = pltpu.SemaphoreType.DMA
    return pl.pallas_call(
        functools.partial(kernel, slots, tile),
        out_shape=jax.ShapeDtypeStruct((toks, width), BF16),
        in_specs=[hbm] * 6,
        out_specs=vmem,
        scratch_shapes=[tok_like, id_like, rw_like,
                        pltpu.VMEM((2, toks, width), BF16), pltpu.VMEM((2, picks, toks), jnp.int32),
                        pltpu.VMEM((2, picks, toks), F32), near_like, pltpu.VMEM((2, mine, width), BF16),
                        all_like, all_like, near_like, pltpu.VMEM((2, mine, width), BF16),
                        pltpu.VMEM((2, toks, width), BF16), tok_like, pltpu.VMEM((toks, width), F32)]
        + [pltpu.VMEM((2 * half, width), BF16)] * 3
        + [pltpu.VMEM((mine, 2 * half), BF16)]
        + [sems((6,)), sems((3,)), sems((3,)), sems((chunks,)), sems((2, chunks)), sems((2,)), sems((2, 2)),
           sems((near,)), sems((near,)), sems((2, near, chunks)), sems((2, 2, chunks)),
           sems((near,)), sems((near,)), sems((2, 2, chunks)), sems((2, near, chunks)),
           sems((2, chunks)), sems((chunks,))],
        compiler_params=pltpu.CompilerParams(
            collective_id=0, has_side_effects=True, vmem_limit_bytes=(53 * 1024 + 512) * 1024),
        cost_estimate=pl.CostEstimate(
            flops=12 * rows * half * width, bytes_accessed=6 * half * width + 4 * toks * width,
            transcendentals=2 * rows * half),
    )(tokens, expert_ids.T, route_weights.T, gate_weight, up_weight, down_weight)


def solution(mesh):
    in_specs = (
        P(("groups", "wide"), "narrow"),
        P(("groups", "wide"), None),
        P(("groups", "wide"), None),
        P("wide", "narrow", None),
        P("wide", "narrow", None),
        P("wide", "narrow", None),
    )
    out_specs = P(("groups", "wide"), "narrow")
    whole_rows = mesh.shape["narrow"] == 1 and mesh.shape["wide"] == 16
    return jax.shard_map(
        fused if whole_rows else per_device, mesh=mesh, in_specs=in_specs, out_specs=out_specs, check_vma=False
    )
```
